256 devices in a mesh: dp: 8 (over x, core), mp: 32 (over y, z).
Axes of the slice: x: 4, y: 4, z: 8, core: 2. Of those that a mesh axis runs over, the one named last changes fastest.
Arguments:
- inputs: bfloat16 [1536, 8192], P('dp', 'mp'), may hold values from -6 to 6
- out_grad: bfloat16 [1536, 8192], P('dp', 'mp'), may hold values from -6 to 6
- frozen_gu: bfloat16 [2, 8192, 16384], P(None, 'dp', 'mp'), may hold values from -0.0625 to 0.0625
- left_gu: bfloat16 [2, 8192, 32], replicated, may hold values from -0.0625 to 0.0625
- right_gu: bfloat16 [2, 32, 16384], P(None, None, 'mp'), may hold values from -0.29882812 to 0.29882812
- magnitude_gu: float32 [2, 16384], P(None, 'mp'), may hold values from 0.5 to 2
- frozen_down: bfloat16 [16384, 8192], P('mp'), may hold values from -0.046875 to 0.046875
- left_down: bfloat16 [16384, 32], P('mp'), may hold values from -0.046875 to 0.046875
- right_down: bfloat16 [32, 8192], replicated, may hold values from -0.29882812 to 0.29882812
- magnitude_down: float32 [8192], replicated, may hold values from 0.5 to 2
Outputs:
- grad_inputs: bfloat16 [1536, 8192], P('dp', 'mp')
- grad_mag_gu: float32 [2, 16384], P(None, 'mp')
- grad_left_gu: float32 [2, 8192, 32], P(None, 'mp')
- grad_right_gu: float32 [2, 32, 16384], P(None, None, 'mp')
- grad_mag_down: float32 [8192], P('mp')
- grad_left_down: float32 [16384, 32], P('mp')
- grad_right_down: float32 [32, 8192], P(None, 'mp')
The draws below stay inside these ranges and needn't reach their ends.
All inputs are finite; a program needn't handle non-finite values.
Results may differ from the reference program's by a relative error of at most 0.0078.
Values may be sent and summed in bfloat16 or wider, within the bound.
No kernel may reach another device: no remote copies, remote signals or barrier semaphores. Data moves between devices by JAX's collectives and lax.ppermute only.
A program may use at most 192 MiB of HBM per device.

```python
import math
import jax
import jax.numpy as jnp
from jax import lax

D = 8192
FW = 16384
R = 32
TOKENS = 1536


def block_scale(own_key, dims, pieces, low, largest):
    loudness, own = 1.0, jax.random.fold_in(own_key, 6)
    for dim, parts in pieces:
        heights = jnp.exp(jax.random.uniform(jax.random.fold_in(own, dim), (parts,), jnp.float32, low / len(pieces), largest / len(pieces)))
        loudness = loudness * jnp.repeat(heights, dims[dim] // parts).reshape([-1 if axis == dim else 1 for axis in range(len(dims))])
    return loudness


def bell_draw(key, dims, deviation, reach, cuts=(), dtype=jnp.bfloat16):
    entries = jax.random.normal(key, dims, jnp.float32) * deviation
    if len(cuts) > 0:
        entries = block_scale(key, dims, cuts, -0.22, 0.18) * entries
    return jnp.clip(entries, min=-reach, max=reach).astype(dtype)


def setup_inputs(seed: int = 0) -> dict:
    keys = jax.random.split(jax.random.key(seed), 11)
    return {
        "inputs": bell_draw(keys[0], (TOKENS, D), 1.0, 6.0, ((0, 8), (1, 32))),
        "out_grad": bell_draw(keys[1], (TOKENS, D), 1.0, 6.0, ((0, 8), (1, 32))),
        "frozen_gu": bell_draw(keys[2], (2, D, FW), D ** -0.5, 0.0625, ((1, 8), (2, 32))),
        "left_gu": bell_draw(keys[3], (2, D, R), D ** -0.5, 0.0625),
        "right_gu": bell_draw(keys[4], (2, R, FW), 0.05, 0.29882812, ((2, 32),)),
        "magnitude_gu": jnp.clip(jnp.exp(math.log(2.0) - 1.3862944 * jax.random.uniform(keys[5], (2, FW), jnp.float32) ** block_scale(keys[5], (2, FW), ((1, 32),), -0.2, 0.2)), 0.5, 2.0),
        "frozen_down": bell_draw(keys[6], (FW, D), FW ** -0.5, 0.046875, ((0, 32),)),
        "left_down": bell_draw(keys[7], (FW, R), FW ** -0.5, 0.046875, ((0, 32),)),
        "right_down": bell_draw(keys[8], (R, D), 0.05, 0.29882812),
        "magnitude_down": jnp.clip(jnp.exp(jax.random.uniform(keys[9], (D,), jnp.float32, math.log(0.5), math.log(2.0))), 0.5, 2.0),
    }


def reference(inputs, out_grad, frozen_gu, left_gu, right_gu, magnitude_gu, frozen_down, left_down, right_down, magnitude_down):
    highest = lax.Precision.HIGHEST
    merged_gu = frozen_gu.astype(jnp.float32) + 2.0 * jnp.einsum('kir,krj->kij', left_gu.astype(jnp.float32), right_gu.astype(jnp.float32), precision=highest)
    norm_gu = jnp.sqrt(lax.optimization_barrier(jnp.sum(merged_gu * merged_gu, axis=1)) + 1e-06)
    tile_gu = merged_gu.astype(jnp.bfloat16)
    merged_down = frozen_down.astype(jnp.float32) + 2.0 * jnp.dot(left_down, right_down, preferred_element_type=jnp.float32)
    norm_down = jnp.sqrt(lax.optimization_barrier(jnp.sum(merged_down * merged_down, axis=0)) + 1e-06)
    tile_down = merged_down.astype(jnp.bfloat16)
    scale_gu = magnitude_gu / norm_gu
    scale_down = magnitude_down / norm_down
    pre_gate = jnp.dot(inputs, tile_gu[0], preferred_element_type=jnp.float32)
    pre_up = jnp.dot(inputs, tile_gu[1], preferred_element_type=jnp.float32)
    hid_gate = pre_gate * scale_gu[0][None, :]
    hid_up = pre_up * scale_gu[1][None, :]
    sig = jax.nn.sigmoid(hid_gate)
    silu_gate = hid_gate * sig
    act = (silu_gate * hid_up).astype(jnp.bfloat16)
    out_pre = jnp.dot(act, tile_down, preferred_element_type=jnp.float32)
    dot_down = lax.optimization_barrier(jnp.sum(out_grad.astype(jnp.float32) * out_pre, axis=0))
    grad_pre_down = (out_grad.astype(jnp.float32) * scale_down[None, :]).astype(jnp.bfloat16)
    grad_act = jnp.dot(grad_pre_down, tile_down.T, preferred_element_type=jnp.float32)
    grad_gate = grad_act * hid_up * sig * (1.0 + hid_gate * (1.0 - sig))
    grad_up = grad_act * silu_gate
    dot_gu = jnp.stack([lax.optimization_barrier(jnp.sum(grad_gate * pre_gate, axis=0)), lax.optimization_barrier(jnp.sum(grad_up * pre_up, axis=0))])
    pre_g_gate = (grad_gate * scale_gu[0][None, :]).astype(jnp.bfloat16)
    pre_g_up = (grad_up * scale_gu[1][None, :]).astype(jnp.bfloat16)
    grad_in = jnp.dot(pre_g_gate, tile_gu[0].T, preferred_element_type=jnp.float32) + jnp.dot(pre_g_up, tile_gu[1].T, preferred_element_type=jnp.float32)
    grad_inputs = grad_in.astype(jnp.bfloat16)
    grad_mag_gu = dot_gu / norm_gu
    grad_mag_down = dot_down / norm_down
    pre_g = jnp.stack([pre_g_gate, pre_g_up])
    rows_gu = jnp.einsum('ktf,krf->ktr', pre_g.astype(jnp.float32), right_gu.astype(jnp.float32), precision=highest)
    rows_down = jnp.dot(grad_pre_down, right_down.T, preferred_element_type=jnp.float32)
    proj_gu = jnp.einsum('td,kdr->ktr', inputs.astype(jnp.float32), left_gu.astype(jnp.float32), precision=highest)
    proj_down = jnp.dot(act, left_down, preferred_element_type=jnp.float32)
    in_f = inputs.astype(jnp.float32)
    grad_left_gu = 2.0 * jnp.einsum('td,ktr->kdr', in_f, rows_gu, precision=highest)
    grad_right_gu = 2.0 * jnp.einsum('ktr,ktf->krf', proj_gu, pre_g.astype(jnp.float32), precision=highest)
    grad_left_down = 2.0 * jnp.einsum('tf,tr->fr', act.astype(jnp.float32), rows_down, precision=highest)
    grad_right_down = 2.0 * jnp.einsum('tr,td->rd', proj_down, grad_pre_down.astype(jnp.float32), precision=highest)
    return (grad_inputs, grad_mag_gu, grad_left_gu, grad_right_gu, grad_mag_down, grad_left_down, grad_right_down)
```

```python
import functools

import jax
import jax.numpy as jnp
from jax import lax
from jax.experimental import pallas as pl
from jax.experimental.pallas import tpu as pltpu
from jax.sharding import Mesh, PartitionSpec as P

F32, BF16 = jnp.float32, jnp.bfloat16
DP, MP = ("x", "core"), ("y", "z")
NX, NC, NY, NZ = 4, 2, 4, 8
NDP, NMP = NX * NC, NY * NZ
NT = (((1,), (1,)), ((), ()))
PAR = dict(vmem_limit_bytes=50 * 1024 * 1024)


def ring_gather(block, axis, n):
    up = [(i, (i + 1) % n) for i in range(n)]
    down = [(i, (i - 1) % n) for i in range(n)]
    behind, ahead = [block], [block]
    for _ in range(n // 2 - 1):
        behind.append(lax.ppermute(behind[-1], axis, up))
        ahead.append(lax.ppermute(ahead[-1], axis, down))
    half = block.shape[0] // 2
    far = jnp.concatenate(
        [lax.ppermute(behind[-1][:half], axis, up), lax.ppermute(ahead[-1][half:], axis, down)]
    )
    return jnp.stack(behind[:0:-1] + ahead + [far])


def place_y_first(pos_ref, block):
    y, z = pos_ref[0], pos_ref[1]
    return lax.rem(block // NZ - y + 1 + NY, NY) * NZ + lax.rem(block % NZ - z + 3 + NZ, NZ)


def place_z_first(pos_ref, block):
    y, z = pos_ref[0], pos_ref[1]
    return lax.rem(block % NZ - z + 3 + NZ, NZ) * NY + lax.rem(block // NZ - y + 1 + NY, NY)


def merge_down_body(frozen_ref, left_ref, right_ref, tile_ref, squares_ref):
    merged = frozen_ref[...].astype(F32) + 2.0 * jnp.dot(
        left_ref[...], right_ref[...], preferred_element_type=F32
    )
    tile_ref[...] = merged.astype(BF16)
    rows, cols = merged.shape
    squares = jnp.sum((merged * merged).reshape(rows // 8, 8, cols), axis=0)
    squares_ref[0] = squares[:, : cols // 2]
    squares_ref[1] = squares[:, cols // 2 :]


def merge_down(frozen, left, right):
    f, d = frozen.shape
    return pl.pallas_call(
        merge_down_body,
        grid=(d // 512,),
        in_specs=[
            pl.BlockSpec((f, 512), lambda c: (0, c)),
            pl.BlockSpec((f, 32), lambda c: (0, 0)),
            pl.BlockSpec((32, 512), lambda c: (0, c)),
        ],
        out_specs=[
            pl.BlockSpec((f, 512), lambda c: (0, c)),
            pl.BlockSpec((2, 8, 256), lambda c: (c, 0, 0)),
        ],
        out_shape=[
            jax.ShapeDtypeStruct((f, d), BF16),
            jax.ShapeDtypeStruct((d // 256, 8, 256), F32),
        ],
        compiler_params=pltpu.CompilerParams(**PAR),
        cost_estimate=pl.CostEstimate(flops=2 * f * d * 40, bytes_accessed=4 * f * d, transcendentals=0),
        name="merge_down",
    )(frozen, left, right)


def proj_body(pos_ref, x_ref, left_ref, out_ref):
    c = pl.program_id(0)

    @pl.when(c == 0)
    def _():
        out_ref[...] = jnp.zeros_like(out_ref)

    for h in range(2):
        x = x_ref[place_y_first(pos_ref, 2 * c + h)]
        for k in range(2):
            out_ref[k] += jnp.dot(x, left_ref[k, h * 256 : (h + 1) * 256], preferred_element_type=F32)


def proj_gate_up(pos, x, left):
    n, t, w = x.shape
    return pl.pallas_call(
        proj_body,
        grid_spec=pltpu.PrefetchScalarGridSpec(
            num_scalar_prefetch=1,
            grid=(n // 2,),
            in_specs=[
                pl.BlockSpec((n, t, w), lambda c, p: (0, 0, 0)),
                pl.BlockSpec((2, 2 * w, 32), lambda c, p: (0, c, 0)),
            ],
            out_specs=pl.BlockSpec((2, t, 32), lambda c, p: (0, 0, 0)),
        ),
        out_shape=jax.ShapeDtypeStruct((2, t, 32), F32),
        compiler_params=pltpu.CompilerParams(**PAR),
        cost_estimate=pl.CostEstimate(flops=n * t * w * 128, bytes_accessed=8_000_000, transcendentals=0),
        name="proj_gate_up",
    )(pos, x, left)


def grad_act_body(pos_ref, g_ref, scale_ref, tile_ref, right_ref, out_ref, rows_ref):
    c = pl.program_id(0)

    @pl.when(c == 0)
    def _():
        out_ref[...] = jnp.zeros_like(out_ref)
        rows_ref[...] = jnp.zeros_like(rows_ref)

    for h in range(2):
        g = g_ref[place_z_first(pos_ref, 2 * c + h)].astype(F32)
        g = (g * scale_ref[h]).astype(BF16)
        cols = slice(h * 256, (h + 1) * 256)
        out_ref[...] += lax.dot_general(g, tile_ref[:, cols], NT, preferred_element_type=F32)
        rows_ref[...] += lax.dot_general(g, right_ref[:, cols], NT, preferred_element_type=F32)


def grad_act_rows(pos, g, scale, tile, right):
    n, t, w = g.shape
    f, d = tile.shape
    return pl.pallas_call(
        grad_act_body,
        grid_spec=pltpu.PrefetchScalarGridSpec(
            num_scalar_prefetch=1,
            grid=(n // 2,),
            in_specs=[
                pl.BlockSpec((n, t, w), lambda c, p: (0, 0, 0)),
                pl.BlockSpec((2, 1, w), lambda c, p: (c, 0, 0)),
                pl.BlockSpec((f, 2 * w), lambda c, p: (0, c)),
                pl.BlockSpec((32, 2 * w), lambda c, p: (0, c)),
            ],
            out_specs=[
                pl.BlockSpec((t, f), lambda c, p: (0, 0)),
                pl.BlockSpec((t, 32), lambda c, p: (0, 0)),
            ],
        ),
        out_shape=[jax.ShapeDtypeStruct((t, f), F32), jax.ShapeDtypeStruct((t, 32), F32)],
        compiler_params=pltpu.CompilerParams(**PAR),
        cost_estimate=pl.CostEstimate(flops=2 * t * f * d, bytes_accessed=12_000_000, transcendentals=0),
        name="grad_act",
    )(pos, g, scale, tile, right)


def dot_down_body(pos_ref, g_ref, act_ref, tile_ref, out_ref):
    c = pl.program_id(0)
    out_pre = jnp.dot(act_ref[...], tile_ref[...], preferred_element_type=F32)
    t = out_pre.shape[0]
    for h in range(2):
        g = g_ref[place_z_first(pos_ref, 2 * c + h)].astype(F32)
        both = g * out_pre[:, h * 256 : (h + 1) * 256]
        out_ref[h] = jnp.sum(both.reshape(t // 8, 8, 256), axis=0)


def dot_down_sums(pos, g, act, tile):
    n, t, w = g.shape
    f, d = tile.shape
    return pl.pallas_call(
        dot_down_body,
        grid_spec=pltpu.PrefetchScalarGridSpec(
            num_scalar_prefetch=1,
            grid=(n // 2,),
            in_specs=[
                pl.BlockSpec((n, t, w), lambda c, p: (0, 0, 0)),
                pl.BlockSpec((t, f), lambda c, p: (0, 0)),
                pl.BlockSpec((f, 2 * w), lambda c, p: (0, c)),
            ],
            out_specs=pl.BlockSpec((2, 8, w), lambda c, p: (c, 0, 0)),
        ),
        out_shape=jax.ShapeDtypeStruct((n, 8, w), F32),
        compiler_params=pltpu.CompilerParams(**PAR),
        cost_estimate=pl.CostEstimate(flops=2 * t * f * d, bytes_accessed=12_000_000, transcendentals=0),
        name="dot_down",
    )(pos, g, act, tile)


def gate_up_body(pos_ref, x_ref, frozen_ref, left_ref, right_ref, tile_ref, pre_ref, squares_ref):
    c = pl.program_id(0)

    @pl.when(c == 0)
    def _():
        pre_ref[...] = jnp.zeros_like(pre_ref)
        squares_ref[...] = jnp.zeros_like(squares_ref)

    for h in range(2):
        x = x_ref[place_y_first(pos_ref, 2 * c + h)]
        rows = slice(h * 256, (h + 1) * 256)
        for k in range(2):
            merged = frozen_ref[k, rows].astype(F32) + 2.0 * jnp.dot(
                left_ref[k, rows], right_ref[k], preferred_element_type=F32
            )
            tile = merged.astype(BF16)
            tile_ref[k, rows] = tile
            squares_ref[k] += jnp.sum((merged * merged).reshape(32, 8, -1), axis=0)
            pre_ref[k] += jnp.dot(x, tile, preferred_element_type=F32)


def gate_up(pos, x, frozen, left, right):
    n, t, w = x.shape
    _, d, f = frozen.shape
    return pl.pallas_call(
        gate_up_body,
        grid_spec=pltpu.PrefetchScalarGridSpec(
            num_scalar_prefetch=1,
            grid=(n // 2,),
            in_specs=[
                pl.BlockSpec((n, t, w), lambda c, p: (0, 0, 0)),
                pl.BlockSpec((2, 2 * w, f), lambda c, p: (0, c, 0)),
                pl.BlockSpec((2, 2 * w, 32), lambda c, p: (0, c, 0)),
                pl.BlockSpec((2, 32, f), lambda c, p: (0, 0, 0)),
            ],
            out_specs=[
                pl.BlockSpec((2, 2 * w, f), lambda c, p: (0, c, 0)),
                pl.BlockSpec((2, t, f), lambda c, p: (0, 0, 0)),
                pl.BlockSpec((2, 8, f), lambda c, p: (0, 0, 0)),
            ],
        ),
        out_shape=[
            jax.ShapeDtypeStruct((2, d, f), BF16),
            jax.ShapeDtypeStruct((2, t, f), F32),
            jax.ShapeDtypeStruct((2, 8, f), F32),
        ],
        compiler_params=pltpu.CompilerParams(**PAR),
        cost_estimate=pl.CostEstimate(flops=4 * t * f * d, bytes_accessed=36_000_000, transcendentals=0),
        name="gate_up",
    )(pos, x, frozen, left, right)


def grad_in_body(first, grads_ref, tile_ref, a_ref, b_ref):
    for h in range(2):
        rows = slice(h * 256, (h + 1) * 256)
        out = lax.dot_general(grads_ref[0], tile_ref[0, rows], NT, preferred_element_type=F32)
        out += lax.dot_general(grads_ref[1], tile_ref[1, rows], NT, preferred_element_type=F32)
        out = out.astype(BF16)
        a_ref[0, h] = out[:first]
        b_ref[h, 0] = out[first:]


def grad_in_parts(grads, tile, first):
    _, t, f = grads.shape
    d = tile.shape[1]
    quarter = NZ // 2
    return pl.pallas_call(
        functools.partial(grad_in_body, first),
        grid=(NMP // 2,),
        in_specs=[
            pl.BlockSpec((2, t, f), lambda c: (0, 0, 0)),
            pl.BlockSpec((2, 512, f), lambda c: (0, c, 0)),
        ],
        out_specs=[
            pl.BlockSpec((1, 2, first, 256), lambda c: (c // quarter, c % quarter, 0, 0)),
            pl.BlockSpec((2, 1, t - first, 256), lambda c: (c % quarter, c // quarter, 0, 0)),
        ],
        out_shape=[
            jax.ShapeDtypeStruct((NY, NZ, first, 256), BF16),
            jax.ShapeDtypeStruct((NZ, NY, t - first, 256), BF16),
        ],
        compiler_params=pltpu.CompilerParams(**PAR),
        cost_estimate=pl.CostEstimate(flops=4 * t * f * d, bytes_accessed=20_000_000, transcendentals=0),
        name="grad_in",
    )(grads, tile)


def exchange(parts, axes):
    return lax.all_to_all(parts, axes, 0, 0, tiled=True)


def sum_parts(parts, axes):
    return jnp.sum(exchange(parts, axes).astype(F32), axis=0)


def total(parts, axes):
    own = sum_parts(parts, axes)
    return exchange(jnp.broadcast_to(own[None], parts.shape), axes)


def shards(
    inputs,
    out_grad,
    frozen_gu,
    left_gu,
    right_gu,
    magnitude_gu,
    frozen_down,
    left_down,
    right_down,
    magnitude_down,
):
    tokens, width = inputs.shape
    iy, iz = lax.axis_index("y"), lax.axis_index("z")
    pos = jnp.stack([iy, iz]).astype(jnp.int32)
    frozen_full = lax.all_gather(frozen_gu, DP, axis=1, tiled=True)

    x_blocks = ring_gather(ring_gather(inputs, "z", NZ), "y", NY).reshape(NMP, tokens, width)
    g_blocks = ring_gather(ring_gather(out_grad, "y", NY), "z", NZ).reshape(NMP, tokens, width)

    tile_down, down_squares = merge_down(frozen_down, left_down, right_down)
    down_sum = jnp.sum(sum_parts(down_squares, MP), axis=0)
    down_sums = exchange(jnp.broadcast_to(down_sum, down_squares.shape), MP)[:, :1]
    norm_down = jnp.sqrt(down_sums + 1e-06)
    scale_down = magnitude_down.reshape(NMP, 1, width) / norm_down
    grad_act, rows_down = grad_act_rows(pos, g_blocks, scale_down, tile_down, right_down)
    proj_gu = proj_gate_up(pos, x_blocks, left_gu)

    tile_gu, pre_gu, gu_squares = gate_up(pos, x_blocks, frozen_full, left_gu, right_gu)
    norm_gu = jnp.sqrt(jnp.sum(gu_squares, axis=1) + 1e-06)
    scale_gu = magnitude_gu / norm_gu
    hid_gu = pre_gu * scale_gu[:, None, :]
    sig = jax.nn.sigmoid(hid_gu[0])
    silu_gate = hid_gu[0] * sig
    act = (silu_gate * hid_gu[1]).astype(BF16)
    grad_gate = grad_act * hid_gu[1] * sig * (1.0 + hid_gu[0] * (1.0 - sig))
    grad_up = grad_act * silu_gate
    grad_hid = jnp.stack([grad_gate, grad_up])
    dot_gu = jnp.sum(grad_hid * pre_gu, axis=1)
    pre_grads = (grad_hid * scale_gu[:, None, :]).astype(BF16)

    rows_gu = jnp.einsum("ktf,krf->tkr", pre_grads, right_gu, preferred_element_type=F32)
    proj_down = jnp.dot(act, left_down, preferred_element_type=F32)
    rows = jnp.concatenate([rows_gu.reshape(tokens, 64), proj_down], axis=1)
    rows = jnp.pad(rows, ((0, 256 - tokens), (0, 32))).reshape(NMP, 8, 128)

    part_a, part_b = grad_in_parts(pre_grads, tile_gu, 128)
    half_a = sum_parts(part_a, "y").astype(BF16)
    half_b = sum_parts(part_b, "z").astype(BF16)
    grad_in = jnp.concatenate([sum_parts(half_a, "z"), sum_parts(half_b, "y")])

    rows = total(rows, MP).reshape(256, 128)[:tokens]
    own = lax.dynamic_index_in_dim(scale_down, iy * NZ + iz, 0, keepdims=False)
    own_norm = lax.dynamic_index_in_dim(norm_down, iy * NZ + iz, 0, keepdims=False)
    own_grads = (out_grad.astype(F32) * own).astype(BF16)
    rows16 = rows.astype(BF16)
    tn = (((0,), (0,)), ((), ()))
    left_gu_part = lax.dot_general(rows16[:, :64], inputs, tn, preferred_element_type=F32)
    right_down_part = lax.dot_general(rows16[:, 64:96], own_grads, tn, preferred_element_type=F32)
    dot_down = jnp.sum(sum_parts(dot_down_sums(pos, g_blocks, act, tile_down), MP), axis=0)

    right_gu_part = jnp.einsum("ktr,ktf->krf", proj_gu.astype(BF16), pre_grads, preferred_element_type=F32)
    left_down_part = lax.dot_general(rows_down.astype(BF16), act, tn, preferred_element_type=F32)
    hidden = pre_gu.shape[2]
    early = jnp.concatenate(
        [2.0 * right_gu_part.reshape(64, hidden), 2.0 * left_down_part, dot_gu, jnp.zeros((30, hidden), F32)]
    )
    early = total(early.reshape(NDP, 16, hidden), DP).reshape(128, hidden)
    late = jnp.concatenate(
        [2.0 * left_gu_part, 2.0 * right_down_part, dot_down[None], jnp.zeros((31, width), F32)]
    )
    late = total(late.reshape(NDP, 16, width), DP).reshape(128, width)
    return (
        grad_in.astype(BF16),
        early[96:98] / norm_gu,
        late[:64].reshape(2, 32, width).swapaxes(1, 2),
        early[:64].reshape(2, 32, hidden),
        late[96] / own_norm[0],
        early[64:96].T,
        late[64:96],
    )


def solution(mesh):
    fine = Mesh(mesh.devices.reshape(NX, NC, NY, NZ), ("x", "core", "y", "z"))
    in_specs = (
        P(DP, MP),
        P(DP, MP),
        P(None, DP, MP),
        P(),
        P(None, None, MP),
        P(None, MP),
        P(MP, None),
        P(MP, None),
        P(),
        P(),
    )
    out_specs = (
        P(DP, MP),
        P(None, MP),
        P(None, MP, None),
        P(None, None, MP),
        P(MP),
        P(MP, None),
        P(None, MP),
    )
    return jax.shard_map(shards, mesh=fine, in_specs=in_specs, out_specs=out_specs, check_vma=False)
```

```python
import functools

import jax
import jax.numpy as jnp
from jax import lax
from jax.experimental import pallas as pl
from jax.experimental.pallas import tpu as pltpu
from jax.sharding import Mesh, PartitionSpec as P

F32, BF16 = jnp.float32, jnp.bfloat16
DP, MP, CMP = ("x", "core"), ("y", "z"), ("core", "y", "z")
NX, NC, NY, NZ = 4, 2, 4, 8
NDP, NMP = NX * NC, NY * NZ
NT = (((1,), (1,)), ((), ()))
TN = (((0,), (0,)), ((), ()))
OTHER = [(0, 1), (1, 0)]
VMEM = 50 * 1024 * 1024


def step(array, axis, n, shift):
    return lax.ppermute(array, axis, [(i, (i + shift) % n) for i in range(n)])


def both_ways(a, b, axis, n):
    return step(a, axis, n, 1), step(b, axis, n, -1)


def nothing(*refs):
    pass


def after(array, *others):
    anywhere = pl.BlockSpec(memory_space=pl.ANY)
    return pl.pallas_call(
        nothing,
        in_specs=[anywhere] * (1 + len(others)),
        out_specs=anywhere,
        out_shape=jax.ShapeDtypeStruct(array.shape, array.dtype),
        input_output_aliases={0: 0},
        name="after",
    )(array, *others)


def stack_body(*refs):
    *pieces, first, second, out = refs
    for i, piece in enumerate(pieces):
        out[i] = piece[...]
    half = first.shape[0]
    out[len(pieces), :half] = first[...]
    out[len(pieces), half:] = second[...]


def stack(pieces, first, second):
    return pl.pallas_call(
        stack_body,
        out_shape=jax.ShapeDtypeStruct((len(pieces) + 1,) + pieces[0].shape, BF16),
        compiler_params=pltpu.CompilerParams(vmem_limit_bytes=VMEM),
        cost_estimate=pl.CostEstimate(flops=0, bytes_accessed=6_000_000, transcendentals=0),
        name="stack",
    )(*pieces, first, second)


def rel(a, b, shift, n):
    return lax.rem(a - b + shift + n, n)


def call(body, name, grid, in_specs, out_specs, out_shape, aliases=None):
    return pl.pallas_call(
        body,
        grid_spec=pltpu.PrefetchScalarGridSpec(
            num_scalar_prefetch=1, grid=grid, in_specs=in_specs, out_specs=out_specs
        ),
        out_shape=out_shape,
        input_output_aliases=aliases or {},
        compiler_params=pltpu.CompilerParams(vmem_limit_bytes=VMEM),
        cost_estimate=pl.CostEstimate(flops=1_000_000_000, bytes_accessed=16_000_000, transcendentals=0),
        name=name,
    )


def merge_down_body(pos_ref, frozen_ref, left_ref, right_ref, tile_ref, squares_ref):
    merged = frozen_ref[...].astype(F32) + 2.0 * lax.dot_general(
        left_ref[...], right_ref[...], TN, preferred_element_type=F32
    )
    tile_ref[...] = merged.astype(BF16)
    rows, cols = merged.shape
    squares = jnp.sum((merged * merged).reshape(rows // 8, 8, cols), axis=0)
    for i in range(cols // 128):
        squares_ref[i] = squares[:, i * 128 : (i + 1) * 128]


def merge_down(pos, frozen, left, right):
    f, d = frozen.shape[0] // NC, frozen.shape[1]
    w = d // NY
    return call(
        merge_down_body,
        "merge_down",
        (NY,),
        [
            pl.BlockSpec((f, w), lambda i, p: (p[1], i)),
            pl.BlockSpec((32, f), lambda i, p: (0, p[1])),
            pl.BlockSpec((32, w), lambda i, p: (0, i)),
        ],
        [
            pl.BlockSpec((f, w), lambda i, p: (0, i)),
            pl.BlockSpec((w // 128, 8, 128), lambda i, p: (i, 0, 0)),
        ],
        [
            jax.ShapeDtypeStruct((f, d), BF16),
            jax.ShapeDtypeStruct((d // 128, 8, 128), F32),
        ],
    )(pos, frozen, left, right)


def x_spec(t, w):
    return pl.BlockSpec((1, NZ, t, w), lambda i, p: (rel(i, p[2], 1, NY), 0, 0, 0))


def g_spec(t, w):
    return pl.BlockSpec((NZ, 1, t, w), lambda i, p: (0, rel(i, p[2], 1, NY), 0, 0))


def proj_body(pos_ref, own_ref, other_ref, left_ref, out_ref):
    @pl.when(pl.program_id(0) == 0)
    def _():
        out_ref[...] = jnp.zeros_like(out_ref)

    total = jnp.zeros(out_ref.shape, F32)
    for i in range(NZ):
        x = jnp.concatenate([own_ref[0, i], other_ref[0, i]])
        cols = slice(i * 256, (i + 1) * 256)
        left = jnp.concatenate([left_ref[0, :, cols], left_ref[1, :, cols]])
        total += lax.dot_general(x, left, NT, preferred_element_type=F32)
    out_ref[...] += total


def proj_gate_up(pos, own, other, left):
    _, _, t, w = own.shape
    return call(
        proj_body,
        "proj_gate_up",
        (NY,),
        [x_spec(t, w), x_spec(t, w), pl.BlockSpec((2, 32, NZ * w), lambda i, p: (0, 0, i))],
        pl.BlockSpec((2 * t, 64), lambda i, p: (0, 0)),
        jax.ShapeDtypeStruct((2 * t, 64), F32),
    )(pos, own, other, left)


def grad_act_body(pos_ref, own_ref, other_ref, scale_ref, tile_ref, right_ref, out_ref, rows_ref):
    @pl.when(pl.program_id(0) == 0)
    def _():
        out_ref[...] = jnp.zeros_like(out_ref)
        rows_ref[...] = jnp.zeros_like(rows_ref)

    total, rows = jnp.zeros(out_ref.shape, F32), jnp.zeros(rows_ref.shape, F32)
    for i in range(NZ):
        q = rel(i, pos_ref[3], 3, NZ)
        g = jnp.concatenate([own_ref[q, 0], other_ref[q, 0]]).astype(F32)
        g = (g * scale_ref[i]).astype(BF16)
        cols = slice(i * 256, (i + 1) * 256)
        total += lax.dot_general(g, tile_ref[:, cols], NT, preferred_element_type=F32)
        rows += lax.dot_general(g, right_ref[:, cols], NT, preferred_element_type=F32)
    out_ref[...] += total
    rows_ref[...] += rows


def grad_act_rows(pos, own, other, scale, tile, right):
    _, _, t, w = own.shape
    f, d = tile.shape
    return call(
        grad_act_body,
        "grad_act",
        (NY,),
        [
            g_spec(t, w),
            g_spec(t, w),
            pl.BlockSpec((NZ, 1, w), lambda i, p: (i, 0, 0)),
            pl.BlockSpec((f, NZ * w), lambda i, p: (0, i)),
            pl.BlockSpec((32, NZ * w), lambda i, p: (0, i)),
        ],
        [
            pl.BlockSpec((2 * t, f), lambda i, p: (0, 0)),
            pl.BlockSpec((2 * t, 32), lambda i, p: (0, 0)),
        ],
        [jax.ShapeDtypeStruct((2 * t, f), F32), jax.ShapeDtypeStruct((2 * t, 32), F32)],
    )(pos, own, other, scale, tile, right)


def dot_down_body(pos_ref, own_ref, other_ref, act_ref, tile_ref, out_ref):
    act = act_ref[...]
    for i in range(NZ):
        q = rel(i, pos_ref[3], 3, NZ)
        g = jnp.concatenate([own_ref[q, 0], other_ref[q, 0]]).astype(F32)
        out_pre = jnp.dot(act, tile_ref[:, i * 256 : (i + 1) * 256], preferred_element_type=F32)
        sums = jnp.sum(g * out_pre, axis=0, keepdims=True)
        out_ref[2 * i] = sums[:, :128]
        out_ref[2 * i + 1] = sums[:, 128:]


def dot_down_sums(pos, own, other, act, tile):
    _, _, t, w = own.shape
    f, d = tile.shape
    return call(
        dot_down_body,
        "dot_down",
        (NY,),
        [
            g_spec(t, w),
            g_spec(t, w),
            pl.BlockSpec((2 * t, f), lambda i, p: (0, 0)),
            pl.BlockSpec((f, NZ * w), lambda i, p: (0, i)),
        ],
        pl.BlockSpec((2 * NZ, 1, 128), lambda i, p: (i, 0, 0)),
        jax.ShapeDtypeStruct((2 * NMP, 1, 128), F32),
    )(pos, own, other, act, tile)


def gate_up_body(pos_ref, own_ref, other_ref, frozen_ref, left_ref, right_ref, tile_ref, pre_ref, squares_ref):
    @pl.when(pl.program_id(0) == 0)
    def _():
        pre_ref[...] = jnp.zeros_like(pre_ref)
        squares_ref[...] = jnp.zeros_like(squares_ref)

    for k in range(2):
        right = right_ref[k]
        pre, squares = jnp.zeros(pre_ref.shape[1:], F32), jnp.zeros(squares_ref.shape[1:], F32)
        for i in range(NZ):
            x = jnp.concatenate([own_ref[0, i], other_ref[0, i]])
            rows = slice(i * 256, (i + 1) * 256)
            merged = frozen_ref[k, rows].astype(F32) + 2.0 * lax.dot_general(
                left_ref[k, :, rows], right, TN, preferred_element_type=F32
            )
            tile = merged.astype(BF16)
            tile_ref[k, rows] = tile
            squares += jnp.sum((merged * merged).reshape(32, 8, -1), axis=0)
            pre += jnp.dot(x, tile, preferred_element_type=F32)
        pre_ref[k] += pre
        squares_ref[k] += squares


def gate_up(pos, own, other, frozen, left, right):
    _, _, t, w = own.shape
    _, d, f = frozen.shape
    f, rows = f // NC, NZ * w
    return call(
        gate_up_body,
        "gate_up",
        (NY,),
        [
            x_spec(t, w),
            x_spec(t, w),
            pl.BlockSpec((2, rows, f), lambda i, p: (0, i, p[1])),
            pl.BlockSpec((2, 32, rows), lambda i, p: (0, 0, i)),
            pl.BlockSpec((2, 32, f), lambda i, p: (0, 0, 0)),
        ],
        [
            pl.BlockSpec((2, rows, f), lambda i, p: (0, i, 0)),
            pl.BlockSpec((2, 2 * t, f), lambda i, p: (0, 0, 0)),
            pl.BlockSpec((2, 8, f), lambda i, p: (0, 0, 0)),
        ],
        [
            jax.ShapeDtypeStruct((2, d, f), BF16),
            jax.ShapeDtypeStruct((2, 2 * t, f), F32),
            jax.ShapeDtypeStruct((2, 8, f), F32),
        ],
    )(pos, own, other, frozen, left, right)


def grad_in_body(pos_ref, grads_ref, tile_ref, own_ref, other_ref):
    t = grads_ref.shape[1] // 2
    for i in range(NZ):
        rows = slice(i * 256, (i + 1) * 256)
        out = lax.dot_general(grads_ref[0], tile_ref[0, rows], NT, preferred_element_type=F32)
        out += lax.dot_general(grads_ref[1], tile_ref[1, rows], NT, preferred_element_type=F32)
        out = out.astype(BF16)
        own_ref[0, i] = out[:t]
        other_ref[0, i] = out[t:]


def grad_in_parts(pos, grads, tiles):
    _, t, f = grads.shape
    out = pl.BlockSpec((1, NZ, t // 2, 256), lambda i, p: (i, 0, 0, 0))
    shape = jax.ShapeDtypeStruct((NY, NZ, t // 2, 256), BF16)
    return call(
        grad_in_body,
        "grad_in",
        (NY,),
        [
            pl.BlockSpec((2, t, f), lambda i, p: (0, 0, 0)),
            pl.BlockSpec((2, NZ * 256, f), lambda i, p: (0, i, 0)),
        ],
        [out, out],
        [shape, shape],
    )(pos, grads, tiles)


def exchange(parts, axes):
    return lax.all_to_all(parts, axes, 0, 0, tiled=True)


def sum_parts(parts, axes):
    return jnp.sum(exchange(parts, axes).astype(F32), axis=0)


def gather_small(own, axes, n):
    return exchange(jnp.broadcast_to(own[None], (n,) + own.shape), axes)


def shards(
    inputs,
    out_grad,
    frozen_gu,
    left_gu,
    right_gu,
    magnitude_gu,
    frozen_down,
    left_down,
    right_down,
    magnitude_down,
):
    tokens, width = inputs.shape
    hidden = frozen_gu.shape[2] // NC
    ix, ic, iy, iz = (lax.axis_index(a) for a in ("x", "core", "y", "z"))
    pos = jnp.stack([ix, ic, iy, iz]).astype(jnp.int32)

    def half_of(array, core, axis):
        return lax.dynamic_slice_in_dim(array, core * hidden, hidden, axis)

    frozen_full = lax.all_gather(frozen_gu, DP, axis=1, tiled=True)
    tile_down, down_squares = merge_down(pos, frozen_down, left_down.T, right_down)
    down_sum = jnp.sum(sum_parts(down_squares, CMP), axis=0, keepdims=True)
    g_y = jnp.stack(
        [step(out_grad, "y", NY, 1), out_grad, step(out_grad, "y", NY, -1), step(out_grad, "y", NY, 2)]
    )
    copies = after(jnp.broadcast_to(inputs[None], (NZ, tokens, width)), down_sum)
    x_z = exchange(copies, "z")
    yr, yl = both_ways(x_z, x_z, "y", NY)
    down_sums = gather_small(jnp.broadcast_to(down_sum, (8, 128)), CMP, NC * NMP)[:, :1]
    yr = after(yr, yl, down_sums)
    yfr, yfl = both_ways(yr[: NZ // 2], yl[NZ // 2 :], "y", NY)
    x_own = stack([yr, x_z, yl], yfr, yfl)
    r1, l1 = both_ways(g_y, g_y, "z", NZ)
    r2, l2 = both_ways(r1, l1, "z", NZ)
    r3, l3 = both_ways(r2, l2, "z", NZ)
    zfr, zfl = both_ways(r3[: NY // 2], l3[NY // 2 :], "z", NZ)
    g_own = stack([r3, r2, r1, g_y, l1, l2, l3], zfr, zfl)
    x_other = lax.ppermute(x_own, "core", OTHER)
    g_other = lax.ppermute(g_own, "core", OTHER)
    right = half_of(right_gu, ic, 2)
    left_t = left_gu.swapaxes(1, 2)

    norm_down = jnp.sqrt(down_sums.reshape(NMP, 1, width) + 1e-06)
    scale_down = magnitude_down.reshape(NMP, 1, width) / norm_down
    grad_act, rows_down = grad_act_rows(pos, g_own, g_other, scale_down, tile_down, right_down)

    proj_gu = proj_gate_up(pos, x_own, x_other, left_t).astype(BF16)
    tiles, pre_gu, squares = gate_up(pos, x_own, x_other, frozen_full, left_t, right)
    norm_gu = jnp.sqrt(jnp.sum(squares, axis=1) + 1e-06)
    scale_gu = half_of(magnitude_gu, ic, 1) / norm_gu
    hid_gu = pre_gu * scale_gu[:, None, :]
    sig = jax.nn.sigmoid(hid_gu[0])
    silu_gate = hid_gu[0] * sig
    act = (silu_gate * hid_gu[1]).astype(BF16)
    grad_gate = grad_act * hid_gu[1] * sig * (1.0 + hid_gu[0] * (1.0 - sig))
    grad_up = grad_act * silu_gate
    grad_hid = jnp.stack([grad_gate, grad_up])
    dot_gu = jnp.sum(grad_hid * pre_gu, axis=1) / norm_gu
    pre_grads = (grad_hid * scale_gu[:, None, :]).astype(BF16)

    own_terms, other_terms = grad_in_parts(pos, pre_grads, tiles)
    from_other = lax.ppermute(other_terms, "core", OTHER)
    terms = (own_terms.astype(F32) + from_other.astype(F32)).astype(BF16)
    grad_in = lax.psum_scatter(lax.psum_scatter(terms, "y").astype(F32), "z")

    rows_gu = [
        lax.dot_general(pre_grads[k], right[k], NT, preferred_element_type=F32) for k in range(2)
    ]
    proj_down = jnp.dot(act, half_of(left_down, ic, 0), preferred_element_type=F32)
    rows = jnp.concatenate(rows_gu + [proj_down, jnp.zeros_like(proj_down)], axis=1)
    rows = rows.reshape(NC, NMP, tokens // NMP, 128)
    rows = jnp.where(ic == 0, rows, rows[::-1]).reshape(NC * NMP, tokens // NMP, 128)
    dots = dot_down_sums(pos, g_own, g_other, act, tile_down)
    rows = jnp.concatenate([rows, dots, jnp.zeros_like(dots)], axis=1)
    rows = gather_small(sum_parts(rows, CMP), CMP, NC * NMP)
    dots = lax.dynamic_slice_in_dim(rows[:, 6], 2 * (iy * NZ + iz), 2, 0).reshape(1, width)
    rows = lax.dynamic_slice_in_dim(rows[:, :6], ic * NMP, NMP, 0).reshape(tokens, 128).astype(BF16)
    own = iy * NZ + iz
    own_scale = lax.dynamic_index_in_dim(scale_down, own, 0, keepdims=False)
    own_norm = lax.dynamic_index_in_dim(norm_down, own, 0, keepdims=False)
    own_grads = (out_grad.astype(F32) * own_scale).astype(BF16)
    left_gu_part = lax.dot_general(rows[:, :64], inputs, TN, preferred_element_type=F32)
    right_down_part = lax.dot_general(rows[:, 64:96], own_grads, TN, preferred_element_type=F32)

    right_gu_parts = [
        lax.dot_general(proj_gu[:, 32 * k : 32 * k + 32], pre_grads[k], TN, preferred_element_type=F32)
        for k in range(2)
    ]
    left_down_part = lax.dot_general(rows_down.astype(BF16), act, TN, preferred_element_type=F32)
    mine = jnp.concatenate(
        [2.0 * p for p in right_gu_parts] + [2.0 * left_down_part, jnp.pad(dot_gu, ((0, 30), (0, 0)))]
    )
    cores = [jnp.where(ic == c, mine, 0.0) for c in range(NC)]
    sums = jnp.concatenate(
        [2.0 * left_gu_part, 2.0 * right_down_part, jnp.pad(0.5 * dots, ((0, 31), (0, 0)))] + cores
    )
    sums = gather_small(sum_parts(sums.reshape(NDP, 48, width), DP), DP, NDP).reshape(384, width)
    cores = sums[128:].reshape(NC, 128, hidden).swapaxes(0, 1).reshape(128, NC * hidden)
    return (
        grad_in.astype(BF16),
        cores[96:98],
        sums[:64].reshape(2, 32, width).swapaxes(1, 2),
        cores[:64].reshape(2, 32, NC * hidden),
        sums[96] / own_norm[0],
        cores[64:96].T,
        sums[64:96],
    )


def solution(mesh):
    fine = Mesh(mesh.devices.reshape(NX, NC, NY, NZ), ("x", "core", "y", "z"))
    in_specs = (
        P(DP, MP),
        P(DP, MP),
        P(None, DP, MP),
        P(),
        P(None, None, MP),
        P(None, MP),
        P(MP, None),
        P(MP, None),
        P(),
        P(),
    )
    out_specs = (
        P(DP, MP),
        P(None, MP),
        P(None, MP, None),
        P(None, None, MP),
        P(MP),
        P(MP, None),
        P(None, MP),
    )
    return jax.shard_map(shards, mesh=fine, in_specs=in_specs, out_specs=out_specs, check_vma=False)
```

```python
import functools

import jax
import jax.numpy as jnp
from jax import lax
from jax.experimental import pallas as pl
from jax.experimental.pallas import tpu as pltpu
from jax.sharding import Mesh, PartitionSpec as P

F32, BF16 = jnp.float32, jnp.bfloat16
DP, MP, CMP = ("x", "core"), ("y", "z"), ("core", "y", "z")
NX, NC, NY, NZ = 4, 2, 4, 8
NDP, NMP = NX * NC, NY * NZ
NT = (((1,), (1,)), ((), ()))
TN = (((0,), (0,)), ((), ()))
OTHER = [(0, 1), (1, 0)]
VMEM = 50 * 1024 * 1024


def step(array, axis, n, shift):
    return lax.ppermute(array, axis, [(i, (i + shift) % n) for i in range(n)])


def both_ways(a, b, axis, n):
    return step(a, axis, n, 1), step(b, axis, n, -1)


def nothing(*refs):
    pass


def after(array, *others):
    anywhere = pl.BlockSpec(memory_space=pl.ANY)
    return pl.pallas_call(
        nothing,
        in_specs=[anywhere] * (1 + len(others)),
        out_specs=anywhere,
        out_shape=jax.ShapeDtypeStruct(array.shape, array.dtype),
        input_output_aliases={0: 0},
        name="after",
    )(array, *others)


def stack_body(*refs):
    *pieces, first, second, out = refs
    for i, piece in enumerate(pieces):
        out[i] = piece[...]
    half = first.shape[0]
    out[len(pieces), :half] = first[...]
    out[len(pieces), half:] = second[...]


def stack(pieces, first, second):
    return pl.pallas_call(
        stack_body,
        out_shape=jax.ShapeDtypeStruct((len(pieces) + 1,) + pieces[0].shape, BF16),
        compiler_params=pltpu.CompilerParams(vmem_limit_bytes=VMEM),
        cost_estimate=pl.CostEstimate(flops=0, bytes_accessed=6_000_000, transcendentals=0),
        name="stack",
    )(*pieces, first, second)


def rel(a, b, shift, n):
    return lax.rem(a - b + shift + n, n)


def call(body, name, grid, in_specs, out_specs, out_shape, aliases=None):
    return pl.pallas_call(
        body,
        grid_spec=pltpu.PrefetchScalarGridSpec(
            num_scalar_prefetch=1, grid=grid, in_specs=in_specs, out_specs=out_specs
        ),
        out_shape=out_shape,
        input_output_aliases=aliases or {},
        compiler_params=pltpu.CompilerParams(vmem_limit_bytes=VMEM),
        cost_estimate=pl.CostEstimate(flops=1_000_000_000, bytes_accessed=16_000_000, transcendentals=0),
        name=name,
    )


def merge_down_body(pos_ref, frozen_ref, left_ref, right_ref, tile_ref, squares_ref):
    merged = frozen_ref[...].astype(F32) + 2.0 * lax.dot_general(
        left_ref[...], right_ref[...], TN, preferred_element_type=F32
    )
    tile_ref[...] = merged.astype(BF16)
    rows, cols = merged.shape
    squares = jnp.sum((merged * merged).reshape(rows // 8, 8, cols), axis=0)
    for i in range(cols // 128):
        squares_ref[i] = squares[:, i * 128 : (i + 1) * 128]


def merge_down(pos, frozen, left, right):
    f, d = frozen.shape[0] // NC, frozen.shape[1]
    w = d // NY
    return call(
        merge_down_body,
        "merge_down",
        (NY,),
        [
            pl.BlockSpec((f, w), lambda i, p: (p[1], i)),
            pl.BlockSpec((32, f), lambda i, p: (0, p[1])),
            pl.BlockSpec((32, w), lambda i, p: (0, i)),
        ],
        [
            pl.BlockSpec((f, w), lambda i, p: (0, i)),
            pl.BlockSpec((w // 128, 8, 128), lambda i, p: (i, 0, 0)),
        ],
        [
            jax.ShapeDtypeStruct((f, d), BF16),
            jax.ShapeDtypeStruct((d // 128, 8, 128), F32),
        ],
    )(pos, frozen, left, right)


def x_spec(t, w):
    return pl.BlockSpec((1, NZ, t, w), lambda i, p: (rel(i, p[2], 1, NY), 0, 0, 0))


def g_spec(t, w):
    return pl.BlockSpec((NZ, 1, t, w), lambda i, p: (0, rel(i, p[2], 1, NY), 0, 0))


def proj_body(pos_ref, own_ref, other_ref, left_ref, out_ref):
    @pl.when(pl.program_id(0) == 0)
    def _():
        out_ref[...] = jnp.zeros_like(out_ref)

    total = jnp.zeros(out_ref.shape, F32)
    for i in range(NZ):
        x = jnp.concatenate([own_ref[0, i], other_ref[0, i]])
        cols = slice(i * 256, (i + 1) * 256)
        left = jnp.concatenate([left_ref[0, :, cols], left_ref[1, :, cols]])
        total += lax.dot_general(x, left, NT, preferred_element_type=F32)
    out_ref[...] += total


def proj_gate_up(pos, own, other, left):
    _, _, t, w = own.shape
    return call(
        proj_body,
        "proj_gate_up",
        (NY,),
        [x_spec(t, w), x_spec(t, w), pl.BlockSpec((2, 32, NZ * w), lambda i, p: (0, 0, i))],
        pl.BlockSpec((2 * t, 64), lambda i, p: (0, 0)),
        jax.ShapeDtypeStruct((2 * t, 64), F32),
    )(pos, own, other, left)


def grad_act_body(pos_ref, own_ref, other_ref, scale_ref, tile_ref, right_ref, out_ref, rows_ref):
    @pl.when(pl.program_id(0) == 0)
    def _():
        out_ref[...] = jnp.zeros_like(out_ref)
        rows_ref[...] = jnp.zeros_like(rows_ref)

    total, rows = jnp.zeros(out_ref.shape, F32), jnp.zeros(rows_ref.shape, F32)
    for i in range(NZ):
        q = rel(i, pos_ref[3], 3, NZ)
        g = jnp.concatenate([own_ref[q, 0], other_ref[q, 0]]).astype(F32)
        g = (g * scale_ref[i]).astype(BF16)
        cols = slice(i * 256, (i + 1) * 256)
        total += lax.dot_general(g, tile_ref[:, cols], NT, preferred_element_type=F32)
        rows += lax.dot_general(g, right_ref[:, cols], NT, preferred_element_type=F32)
    out_ref[...] += total
    rows_ref[...] += rows


def grad_act_rows(pos, own, other, scale, tile, right):
    _, _, t, w = own.shape
    f, d = tile.shape
    return call(
        grad_act_body,
        "grad_act",
        (NY,),
        [
            g_spec(t, w),
            g_spec(t, w),
            pl.BlockSpec((NZ, 1, w), lambda i, p: (i, 0, 0)),
            pl.BlockSpec((f, NZ * w), lambda i, p: (0, i)),
            pl.BlockSpec((32, NZ * w), lambda i, p: (0, i)),
        ],
        [
            pl.BlockSpec((2 * t, f), lambda i, p: (0, 0)),
            pl.BlockSpec((2 * t, 32), lambda i, p: (0, 0)),
        ],
        [jax.ShapeDtypeStruct((2 * t, f), F32), jax.ShapeDtypeStruct((2 * t, 32), F32)],
    )(pos, own, other, scale, tile, right)


def dot_down_body(pos_ref, own_ref, other_ref, act_ref, tile_ref, out_ref):
    act = act_ref[...]
    for i in range(NZ):
        q = rel(i, pos_ref[3], 3, NZ)
        g = jnp.concatenate([own_ref[q, 0], other_ref[q, 0]]).astype(F32)
        out_pre = jnp.dot(act, tile_ref[:, i * 256 : (i + 1) * 256], preferred_element_type=F32)
        sums = jnp.sum(g * out_pre, axis=0, keepdims=True)
        out_ref[2 * i] = sums[:, :128]
        out_ref[2 * i + 1] = sums[:, 128:]


def dot_down_sums(pos, own, other, act, tile):
    _, _, t, w = own.shape
    f, d = tile.shape
    return call(
        dot_down_body,
        "dot_down",
        (NY,),
        [
            g_spec(t, w),
            g_spec(t, w),
            pl.BlockSpec((2 * t, f), lambda i, p: (0, 0)),
            pl.BlockSpec((f, NZ * w), lambda i, p: (0, i)),
        ],
        pl.BlockSpec((2 * NZ, 1, 128), lambda i, p: (i, 0, 0)),
        jax.ShapeDtypeStruct((2 * NMP, 1, 128), F32),
    )(pos, own, other, act, tile)


def gate_up_body(pos_ref, own_ref, other_ref, frozen_ref, left_ref, right_ref, tile_ref, pre_ref, squares_ref):
    @pl.when(pl.program_id(0) == 0)
    def _():
        pre_ref[...] = jnp.zeros_like(pre_ref)
        squares_ref[...] = jnp.zeros_like(squares_ref)

    for k in range(2):
        right = right_ref[k]
        pre, squares = jnp.zeros(pre_ref.shape[1:], F32), jnp.zeros(squares_ref.shape[1:], F32)
        for i in range(NZ):
            x = jnp.concatenate([own_ref[0, i], other_ref[0, i]])
            rows = slice(i * 256, (i + 1) * 256)
            merged = frozen_ref[k, rows].astype(F32) + 2.0 * lax.dot_general(
                left_ref[k, :, rows], right, TN, preferred_element_type=F32
            )
            tile = merged.astype(BF16)
            tile_ref[k, rows] = tile
            squares += jnp.sum((merged * merged).reshape(32, 8, -1), axis=0)
            pre += jnp.dot(x, tile, preferred_element_type=F32)
        pre_ref[k] += pre
        squares_ref[k] += squares


def gate_up(pos, own, other, frozen, left, right):
    _, _, t, w = own.shape
    _, d, f = frozen.shape
    f, rows = f // NC, NZ * w
    return call(
        gate_up_body,
        "gate_up",
        (NY,),
        [
            x_spec(t, w),
            x_spec(t, w),
            pl.BlockSpec((2, rows, f), lambda i, p: (0, i, p[1])),
            pl.BlockSpec((2, 32, rows), lambda i, p: (0, 0, i)),
            pl.BlockSpec((2, 32, f), lambda i, p: (0, 0, 0)),
        ],
        [
            pl.BlockSpec((2, rows, f), lambda i, p: (0, i, 0)),
            pl.BlockSpec((2, 2 * t, f), lambda i, p: (0, 0, 0)),
            pl.BlockSpec((2, 8, f), lambda i, p: (0, 0, 0)),
        ],
        [
            jax.ShapeDtypeStruct((2, d, f), BF16),
            jax.ShapeDtypeStruct((2, 2 * t, f), F32),
            jax.ShapeDtypeStruct((2, 8, f), F32),
        ],
    )(pos, own, other, frozen, left, right)


def grad_in_body(pos_ref, grads_ref, tile_ref, own_ref, other_ref):
    t = grads_ref.shape[1] // 2
    for i in range(NZ):
        rows = slice(i * 256, (i + 1) * 256)
        out = lax.dot_general(grads_ref[0], tile_ref[0, rows], NT, preferred_element_type=F32)
        out += lax.dot_general(grads_ref[1], tile_ref[1, rows], NT, preferred_element_type=F32)
        out = out.astype(BF16)
        own_ref[0, i] = out[:t]
        other_ref[0, i] = out[t:]


def grad_in_parts(pos, grads, tiles):
    _, t, f = grads.shape
    out = pl.BlockSpec((1, NZ, t // 2, 256), lambda i, p: (i, 0, 0, 0))
    shape = jax.ShapeDtypeStruct((NY, NZ, t // 2, 256), BF16)
    return call(
        grad_in_body,
        "grad_in",
        (NY,),
        [
            pl.BlockSpec((2, t, f), lambda i, p: (0, 0, 0)),
            pl.BlockSpec((2, NZ * 256, f), lambda i, p: (0, i, 0)),
        ],
        [out, out],
        [shape, shape],
    )(pos, grads, tiles)


def exchange(parts, axes):
    return lax.all_to_all(parts, axes, 0, 0, tiled=True)


def sum_parts(parts, axes):
    return jnp.sum(exchange(parts, axes).astype(F32), axis=0)


def gather_small(own, axes, n):
    return exchange(jnp.broadcast_to(own[None], (n,) + own.shape), axes)


def shards(
    inputs,
    out_grad,
    frozen_gu,
    left_gu,
    right_gu,
    magnitude_gu,
    frozen_down,
    left_down,
    right_down,
    magnitude_down,
):
    tokens, width = inputs.shape
    hidden = frozen_gu.shape[2] // NC
    ix, ic, iy, iz = (lax.axis_index(a) for a in ("x", "core", "y", "z"))
    pos = jnp.stack([ix, ic, iy, iz]).astype(jnp.int32)

    def half_of(array, core, axis):
        return lax.dynamic_slice_in_dim(array, core * hidden, hidden, axis)

    frozen_full = lax.all_gather(frozen_gu, DP, axis=1, tiled=True)
    g_y = jnp.stack(
        [step(out_grad, "y", NY, 1), out_grad, step(out_grad, "y", NY, -1), step(out_grad, "y", NY, 2)]
    )
    x_z = gather_small(inputs, "z", NZ)
    tile_down, down_squares = merge_down(pos, frozen_down, left_down.T, right_down)
    x_z = after(x_z, down_squares)
    yr, yl = both_ways(x_z, x_z, "y", NY)
    down_sum = jnp.sum(sum_parts(after(down_squares, x_z), CMP), axis=0, keepdims=True)
    yr = after(yr, yl, down_sum)
    yfr, yfl = both_ways(yr[: NZ // 2], yl[NZ // 2 :], "y", NY)
    down_sums = gather_small(jnp.broadcast_to(down_sum, (8, 128)), CMP, NC * NMP)[:, :1]
    x_own = stack([yr, x_z, yl], yfr, yfl)
    r1, l1 = both_ways(g_y, g_y, "z", NZ)
    r2, l2 = both_ways(r1, l1, "z", NZ)
    r3, l3 = both_ways(r2, l2, "z", NZ)
    r3 = after(r3, l3, down_sums)
    zfr, zfl = both_ways(r3[: NY // 2], l3[NY // 2 :], "z", NZ)
    g_own = stack([r3, r2, r1, g_y, l1, l2, l3], zfr, zfl)
    x_other = lax.ppermute(x_own, "core", OTHER)
    g_other = lax.ppermute(g_own, "core", OTHER)
    right = half_of(right_gu, ic, 2)
    left_t = left_gu.swapaxes(1, 2)

    norm_down = jnp.sqrt(down_sums.reshape(NMP, 1, width) + 1e-06)
    scale_down = magnitude_down.reshape(NMP, 1, width) / norm_down
    grad_act, rows_down = grad_act_rows(pos, g_own, g_other, scale_down, tile_down, right_down)

    proj_gu = proj_gate_up(pos, x_own, x_other, left_t).astype(BF16)
    tiles, pre_gu, squares = gate_up(pos, x_own, x_other, frozen_full, left_t, right)
    norm_gu = jnp.sqrt(jnp.sum(squares, axis=1) + 1e-06)
    scale_gu = half_of(magnitude_gu, ic, 1) / norm_gu
    hid_gu = pre_gu * scale_gu[:, None, :]
    sig = jax.nn.sigmoid(hid_gu[0])
    silu_gate = hid_gu[0] * sig
    act = (silu_gate * hid_gu[1]).astype(BF16)
    grad_gate = grad_act * hid_gu[1] * sig * (1.0 + hid_gu[0] * (1.0 - sig))
    grad_up = grad_act * silu_gate
    grad_hid = jnp.stack([grad_gate, grad_up])
    dot_gu = jnp.sum(grad_hid * pre_gu, axis=1) / norm_gu
    pre_grads = (grad_hid * scale_gu[:, None, :]).astype(BF16)

    own_terms, other_terms = grad_in_parts(pos, pre_grads, tiles)
    from_other = lax.ppermute(other_terms, "core", OTHER)

    rows_gu = [
        lax.dot_general(pre_grads[k], right[k], NT, preferred_element_type=F32) for k in range(2)
    ]
    proj_down = jnp.dot(act, half_of(left_down, ic, 0), preferred_element_type=F32)
    rows = jnp.concatenate(rows_gu + [proj_down, jnp.zeros_like(proj_down)], axis=1)
    rows = rows.reshape(NC, NMP, tokens // NMP, 128)
    rows = jnp.where(ic == 0, rows, rows[::-1]).reshape(NC * NMP, tokens // NMP, 128)
    rows = jnp.pad(rows, ((0, 0), (0, 2), (0, 0)))
    from_other = after(from_other, rows)
    terms = (own_terms.astype(F32) + from_other.astype(F32)).astype(BF16)
    over_y = lax.psum_scatter(terms, "y")
    rows = sum_parts(after(rows, terms), CMP)
    dots = dot_down_sums(pos, g_own, g_other, act, tile_down).reshape(NMP, NC, 1, 128)
    dots = dots.swapaxes(0, 1).reshape(NC * NMP, 1, 128)
    rows = jnp.broadcast_to(rows[None, :6], (NC * NMP, 6, 128))
    rows = exchange(jnp.concatenate([rows, dots, jnp.zeros_like(dots)], axis=1), CMP)
    grad_in = lax.psum_scatter(after(over_y, rows).astype(F32), "z")
    dots = jnp.sum(rows[:, 6:7], axis=0)
    dots = jnp.concatenate([jnp.where(ic == c, dots, 0.0) for c in range(NC)], axis=1)
    rows = lax.dynamic_slice_in_dim(rows[:, :6], ic * NMP, NMP, 0).reshape(tokens, 128).astype(BF16)
    own = iy * NZ + iz
    own_scale = lax.dynamic_index_in_dim(scale_down, own, 0, keepdims=False)
    own_norm = lax.dynamic_index_in_dim(norm_down, own, 0, keepdims=False)
    own_grads = (out_grad.astype(F32) * own_scale).astype(BF16)
    left_gu_part = lax.dot_general(rows[:, :64], inputs, TN, preferred_element_type=F32)
    right_down_part = lax.dot_general(rows[:, 64:96], own_grads, TN, preferred_element_type=F32)

    right_gu_parts = [
        lax.dot_general(proj_gu[:, 32 * k : 32 * k + 32], pre_grads[k], TN, preferred_element_type=F32)
        for k in range(2)
    ]
    left_down_part = lax.dot_general(rows_down.astype(BF16), act, TN, preferred_element_type=F32)
    mine = jnp.concatenate(
        [2.0 * p for p in right_gu_parts] + [2.0 * left_down_part, jnp.pad(dot_gu, ((0, 30), (0, 0)))]
    )
    cores = [jnp.where(ic == c, mine, 0.0) for c in range(NC)]
    sums = jnp.concatenate(
        [2.0 * left_gu_part, 2.0 * right_down_part, jnp.pad(dots, ((0, 31), (0, 0)))] + cores
    )
    sums = gather_small(sum_parts(sums.reshape(NDP, 48, width), DP), DP, NDP).reshape(384, width)
    cores = sums[128:].reshape(NC, 128, hidden).swapaxes(0, 1).reshape(128, NC * hidden)
    return (
        grad_in.astype(BF16),
        cores[96:98],
        sums[:64].reshape(2, 32, width).swapaxes(1, 2),
        cores[:64].reshape(2, 32, NC * hidden),
        sums[96] / own_norm[0],
        cores[64:96].T,
        sums[64:96],
    )


def solution(mesh):
    fine = Mesh(mesh.devices.reshape(NX, NC, NY, NZ), ("x", "core", "y", "z"))
    in_specs = (
        P(DP, MP),
        P(DP, MP),
        P(None, DP, MP),
        P(),
        P(None, None, MP),
        P(None, MP),
        P(MP, None),
        P(MP, None),
        P(),
        P(),
    )
    out_specs = (
        P(DP, MP),
        P(None, MP),
        P(None, MP, None),
        P(None, None, MP),
        P(MP),
        P(MP, None),
        P(None, MP),
    )
    return jax.shard_map(shards, mesh=fine, in_specs=in_specs, out_specs=out_specs, check_vma=False)
```

```python
import functools

import jax
import jax.numpy as jnp
from jax import lax
from jax.experimental import pallas as pl
from jax.experimental.pallas import tpu as pltpu
from jax.sharding import Mesh, PartitionSpec as P

F32, BF16 = jnp.float32, jnp.bfloat16
DP, MP, CMP = ("x", "core"), ("y", "z"), ("core", "y", "z")
NX, NC, NY, NZ = 4, 2, 4, 8
NDP, NMP = NX * NC, NY * NZ
NT = (((1,), (1,)), ((), ()))
TN = (((0,), (0,)), ((), ()))
OTHER = [(0, 1), (1, 0)]
VMEM = 50 * 1024 * 1024


def step(array, axis, n, shift):
    return lax.ppermute(array, axis, [(i, (i + shift) % n) for i in range(n)])


def both_ways(a, b, axis, n):
    return step(a, axis, n, 1), step(b, axis, n, -1)


def nothing(*refs):
    pass


def after(array, *others):
    anywhere = pl.BlockSpec(memory_space=pl.ANY)
    return pl.pallas_call(
        nothing,
        in_specs=[anywhere] * (1 + len(others)),
        out_specs=anywhere,
        out_shape=jax.ShapeDtypeStruct(array.shape, array.dtype),
        input_output_aliases={0: 0},
        name="after",
    )(array, *others)


def stack_body(*refs):
    *pieces, first, second, out = refs
    for i, piece in enumerate(pieces):
        out[i] = piece[...]
    half = first.shape[0]
    out[len(pieces), :half] = first[...]
    out[len(pieces), half:] = second[...]


def stack(pieces, first, second):
    return pl.pallas_call(
        stack_body,
        out_shape=jax.ShapeDtypeStruct((len(pieces) + 1,) + pieces[0].shape, BF16),
        compiler_params=pltpu.CompilerParams(vmem_limit_bytes=VMEM),
        cost_estimate=pl.CostEstimate(flops=0, bytes_accessed=6_000_000, transcendentals=0),
        name="stack",
    )(*pieces, first, second)


def rel(a, b, shift, n):
    return lax.rem(a - b + shift + n, n)


def call(body, name, grid, in_specs, out_specs, out_shape, aliases=None):
    return pl.pallas_call(
        body,
        grid_spec=pltpu.PrefetchScalarGridSpec(
            num_scalar_prefetch=1, grid=grid, in_specs=in_specs, out_specs=out_specs
        ),
        out_shape=out_shape,
        input_output_aliases=aliases or {},
        compiler_params=pltpu.CompilerParams(vmem_limit_bytes=VMEM),
        cost_estimate=pl.CostEstimate(flops=1_000_000_000, bytes_accessed=16_000_000, transcendentals=0),
        name=name,
    )


def merge_down_body(pos_ref, frozen_ref, left_ref, right_ref, tile_ref, squares_ref):
    merged = frozen_ref[...].astype(F32) + 2.0 * lax.dot_general(
        left_ref[...], right_ref[...], TN, preferred_element_type=F32
    )
    tile_ref[...] = merged.astype(BF16)
    rows, cols = merged.shape
    squares = jnp.sum((merged * merged).reshape(rows // 8, 8, cols), axis=0)
    for i in range(cols // 128):
        squares_ref[i] = squares[:, i * 128 : (i + 1) * 128]


def merge_down(pos, frozen, left, right):
    f, d = frozen.shape[0] // NC, frozen.shape[1]
    w = d // NY
    return call(
        merge_down_body,
        "merge_down",
        (NY,),
        [
            pl.BlockSpec((f, w), lambda i, p: (p[1], i)),
            pl.BlockSpec((32, f), lambda i, p: (0, p[1])),
            pl.BlockSpec((32, w), lambda i, p: (0, i)),
        ],
        [
            pl.BlockSpec((f, w), lambda i, p: (0, i)),
            pl.BlockSpec((w // 128, 8, 128), lambda i, p: (i, 0, 0)),
        ],
        [
            jax.ShapeDtypeStruct((f, d), BF16),
            jax.ShapeDtypeStruct((d // 128, 8, 128), F32),
        ],
    )(pos, frozen, left, right)


def x_spec(t, w):
    return pl.BlockSpec((1, NZ, t, w), lambda i, p: (rel(i, p[2], 1, NY), 0, 0, 0))


def g_spec(t, w):
    return pl.BlockSpec((NZ, 1, t, w), lambda i, p: (0, rel(i, p[2], 1, NY), 0, 0))


def proj_body(pos_ref, own_ref, other_ref, left_ref, _, out_ref):
    @pl.when(pl.program_id(0) == 0)
    def _():
        out_ref[...] = jnp.zeros_like(out_ref)

    total = jnp.zeros(out_ref.shape, F32)
    for i in range(NZ):
        x = jnp.concatenate([own_ref[0, i], other_ref[0, i]])
        cols = slice(i * 256, (i + 1) * 256)
        left = jnp.concatenate([left_ref[0, :, cols], left_ref[1, :, cols]])
        total += lax.dot_general(x, left, NT, preferred_element_type=F32)
    out_ref[...] += total


def proj_gate_up(pos, own, other, left, before):
    _, _, t, w = own.shape
    return call(
        proj_body,
        "proj_gate_up",
        (NY,),
        [
            x_spec(t, w),
            x_spec(t, w),
            pl.BlockSpec((2, 32, NZ * w), lambda i, p: (0, 0, i)),
            pl.BlockSpec(memory_space=pl.ANY),
        ],
        pl.BlockSpec((2 * t, 64), lambda i, p: (0, 0)),
        jax.ShapeDtypeStruct((2 * t, 64), F32),
    )(pos, own, other, left, before)


def grad_act_body(pos_ref, own_ref, other_ref, scale_ref, tile_ref, right_ref, _, out_ref, rows_ref):
    @pl.when(pl.program_id(0) == 0)
    def _():
        out_ref[...] = jnp.zeros_like(out_ref)
        rows_ref[...] = jnp.zeros_like(rows_ref)

    total, rows = jnp.zeros(out_ref.shape, F32), jnp.zeros(rows_ref.shape, F32)
    for i in range(NZ):
        q = rel(i, pos_ref[3], 3, NZ)
        g = jnp.concatenate([own_ref[q, 0], other_ref[q, 0]]).astype(F32)
        g = (g * scale_ref[i]).astype(BF16)
        cols = slice(i * 256, (i + 1) * 256)
        total += lax.dot_general(g, tile_ref[:, cols], NT, preferred_element_type=F32)
        rows += lax.dot_general(g, right_ref[:, cols], NT, preferred_element_type=F32)
    out_ref[...] += total
    rows_ref[...] += rows


def grad_act_rows(pos, own, other, scale, tile, right, before):
    _, _, t, w = own.shape
    f, d = tile.shape
    return call(
        grad_act_body,
        "grad_act",
        (NY,),
        [
            g_spec(t, w),
            g_spec(t, w),
            pl.BlockSpec((NZ, 1, w), lambda i, p: (i, 0, 0)),
            pl.BlockSpec((f, NZ * w), lambda i, p: (0, i)),
            pl.BlockSpec((32, NZ * w), lambda i, p: (0, i)),
            pl.BlockSpec(memory_space=pl.ANY),
        ],
        [
            pl.BlockSpec((2 * t, f), lambda i, p: (0, 0)),
            pl.BlockSpec((2 * t, 32), lambda i, p: (0, 0)),
        ],
        [jax.ShapeDtypeStruct((2 * t, f), F32), jax.ShapeDtypeStruct((2 * t, 32), F32)],
    )(pos, own, other, scale, tile, right, before)


def dot_down_body(pos_ref, own_ref, other_ref, act_ref, tile_ref, out_ref):
    act = act_ref[...]
    for i in range(NZ):
        q = rel(i, pos_ref[3], 3, NZ)
        g = jnp.concatenate([own_ref[q, 0], other_ref[q, 0]]).astype(F32)
        out_pre = jnp.dot(act, tile_ref[:, i * 256 : (i + 1) * 256], preferred_element_type=F32)
        sums = jnp.sum(g * out_pre, axis=0, keepdims=True)
        out_ref[2 * i] = sums[:, :128]
        out_ref[2 * i + 1] = sums[:, 128:]


def dot_down_sums(pos, own, other, act, tile):
    _, _, t, w = own.shape
    f, d = tile.shape
    return call(
        dot_down_body,
        "dot_down",
        (NY,),
        [
            g_spec(t, w),
            g_spec(t, w),
            pl.BlockSpec((2 * t, f), lambda i, p: (0, 0)),
            pl.BlockSpec((f, NZ * w), lambda i, p: (0, i)),
        ],
        pl.BlockSpec((2 * NZ, 1, 128), lambda i, p: (i, 0, 0)),
        jax.ShapeDtypeStruct((2 * NMP, 1, 128), F32),
    )(pos, own, other, act, tile)


def gate_up_body(
    pos_ref, own_ref, other_ref, frozen_ref, left_ref, right_ref, _, tile_ref, pre_ref, squares_ref
):
    @pl.when(pl.program_id(0) == 0)
    def _():
        pre_ref[...] = jnp.zeros_like(pre_ref)
        squares_ref[...] = jnp.zeros_like(squares_ref)

    for k in range(2):
        right = right_ref[k]
        pre, squares = jnp.zeros(pre_ref.shape[1:], F32), jnp.zeros(squares_ref.shape[1:], F32)
        for i in range(NZ):
            x = jnp.concatenate([own_ref[0, i], other_ref[0, i]])
            rows = slice(i * 256, (i + 1) * 256)
            merged = frozen_ref[k, rows].astype(F32) + 2.0 * lax.dot_general(
                left_ref[k, :, rows], right, TN, preferred_element_type=F32
            )
            tile = merged.astype(BF16)
            tile_ref[k, rows] = tile
            squares += jnp.sum((merged * merged).reshape(32, 8, -1), axis=0)
            pre += jnp.dot(x, tile, preferred_element_type=F32)
        pre_ref[k] += pre
        squares_ref[k] += squares


def gate_up(pos, own, other, frozen, left, right, before):
    _, _, t, w = own.shape
    _, d, f = frozen.shape
    f, rows = f // NC, NZ * w
    return call(
        gate_up_body,
        "gate_up",
        (NY,),
        [
            x_spec(t, w),
            x_spec(t, w),
            pl.BlockSpec((2, rows, f), lambda i, p: (0, i, p[1])),
            pl.BlockSpec((2, 32, rows), lambda i, p: (0, 0, i)),
            pl.BlockSpec((2, 32, f), lambda i, p: (0, 0, 0)),
            pl.BlockSpec(memory_space=pl.ANY),
        ],
        [
            pl.BlockSpec((2, rows, f), lambda i, p: (0, i, 0)),
            pl.BlockSpec((2, 2 * t, f), lambda i, p: (0, 0, 0)),
            pl.BlockSpec((2, 8, f), lambda i, p: (0, 0, 0)),
        ],
        [
            jax.ShapeDtypeStruct((2, d, f), BF16),
            jax.ShapeDtypeStruct((2, 2 * t, f), F32),
            jax.ShapeDtypeStruct((2, 8, f), F32),
        ],
    )(pos, own, other, frozen, left, right, before)


def grad_in_body(pos_ref, grads_ref, tile_ref, *refs):
    *from_ref, out_ref = refs
    for i in range(NZ):
        rows = slice(i * 256, (i + 1) * 256)
        out = lax.dot_general(grads_ref[0], tile_ref[0, rows], NT, preferred_element_type=F32)
        out += lax.dot_general(grads_ref[1], tile_ref[1, rows], NT, preferred_element_type=F32)
        if from_ref:
            out += from_ref[0][i, 0].astype(F32)
        out_ref[i, 0] = out.astype(BF16)


def grad_in_terms(pos, grads, tiles, half, *from_other):
    _, t, f = grads.shape
    t = t // 2
    out = pl.BlockSpec((NZ, 1, t, 256), lambda i, p: (0, i, 0, 0))
    return call(
        grad_in_body,
        "grad_in",
        (NY,),
        [
            pl.BlockSpec((2, t, f), lambda i, p: (0, half, 0)),
            pl.BlockSpec((2, NZ * 256, f), lambda i, p: (0, i, 0)),
        ]
        + [out] * len(from_other),
        out,
        jax.ShapeDtypeStruct((NZ, NY, t, 256), BF16),
    )(pos, grads, tiles, *from_other)


def exchange(parts, axes):
    return lax.all_to_all(parts, axes, 0, 0, tiled=True)


def sum_parts(parts, axes):
    return jnp.sum(exchange(parts, axes).astype(F32), axis=0)


def gather_small(own, axes, n):
    return exchange(jnp.broadcast_to(own[None], (n,) + own.shape), axes)


def shards(
    inputs,
    out_grad,
    frozen_gu,
    left_gu,
    right_gu,
    magnitude_gu,
    frozen_down,
    left_down,
    right_down,
    magnitude_down,
):
    tokens, width = inputs.shape
    hidden = frozen_gu.shape[2] // NC
    ix, ic, iy, iz = (lax.axis_index(a) for a in ("x", "core", "y", "z"))
    pos = jnp.stack([ix, ic, iy, iz]).astype(jnp.int32)

    def half_of(array, core, axis):
        return lax.dynamic_slice_in_dim(array, core * hidden, hidden, axis)

    frozen_full = lax.all_gather(frozen_gu, DP, axis=1, tiled=True)
    g_y = jnp.stack(
        [step(out_grad, "y", NY, 1), out_grad, step(out_grad, "y", NY, -1), step(out_grad, "y", NY, 2)]
    )
    x_z = gather_small(inputs, "z", NZ)
    tile_down, down_squares = merge_down(pos, frozen_down, left_down.T, right_down)
    x_z = after(x_z, down_squares)
    yr, yl = both_ways(x_z, x_z, "y", NY)
    yfr, yfl = both_ways(yr[: NZ // 2], yl[NZ // 2 :], "y", NY)
    x_own = stack([yr, x_z, yl], yfr, yfl)
    r1, l1 = both_ways(g_y, g_y, "z", NZ)
    down_sum = jnp.sum(sum_parts(after(down_squares, r1, l1), CMP), axis=0, keepdims=True)
    r2, l2 = both_ways(r1, l1, "z", NZ)
    r2, l2 = after(r2, down_sum), after(l2, down_sum)
    down_sums = gather_small(jnp.broadcast_to(down_sum, (8, 128)), CMP, NC * NMP)[:, :1]
    r3, l3 = both_ways(r2, l2, "z", NZ)
    r3, l3 = after(r3, down_sums), after(l3, down_sums)
    zfr, zfl = both_ways(r3[: NY // 2], l3[NY // 2 :], "z", NZ)
    x_other = lax.ppermute(x_own, "core", OTHER)
    right = half_of(right_gu, ic, 2)
    left_t = left_gu.swapaxes(1, 2)

    norm_down = jnp.sqrt(down_sums.reshape(NMP, 1, width) + 1e-06)
    scale_down = magnitude_down.reshape(NMP, 1, width) / norm_down

    tiles, pre_gu, squares = gate_up(pos, x_own, x_other, frozen_full, left_t, right, down_sums)
    g_own = stack([r3, r2, r1, g_y, l1, l2, l3], after(zfr, squares), zfl)
    g_other = lax.ppermute(g_own, "core", OTHER)
    proj_gu = proj_gate_up(pos, x_own, x_other, left_t, g_own)
    grad_act, rows_down = grad_act_rows(pos, g_own, g_other, scale_down, tile_down, right_down, proj_gu)
    proj_gu = proj_gu.astype(BF16)
    norm_gu = jnp.sqrt(jnp.sum(squares, axis=1) + 1e-06)
    scale_gu = half_of(magnitude_gu, ic, 1) / norm_gu
    hid_gu = pre_gu * scale_gu[:, None, :]
    sig = jax.nn.sigmoid(hid_gu[0])
    silu_gate = hid_gu[0] * sig
    act = (silu_gate * hid_gu[1]).astype(BF16)
    grad_gate = grad_act * hid_gu[1] * sig * (1.0 + hid_gu[0] * (1.0 - sig))
    grad_up = grad_act * silu_gate
    grad_hid = jnp.stack([grad_gate, grad_up])
    dot_gu = jnp.sum(grad_hid * pre_gu, axis=1) / norm_gu
    pre_grads = (grad_hid * scale_gu[:, None, :]).astype(BF16)

    other_terms = grad_in_terms(pos, pre_grads, tiles, 1)
    from_other = lax.ppermute(other_terms, "core", OTHER)

    rows_gu = [
        lax.dot_general(pre_grads[k], right[k], NT, preferred_element_type=F32) for k in range(2)
    ]
    proj_down = jnp.dot(act, half_of(left_down, ic, 0), preferred_element_type=F32)
    rows = jnp.concatenate(rows_gu + [proj_down, jnp.zeros_like(proj_down)], axis=1)
    rows = rows.reshape(NC, NMP, tokens // NMP, 128)
    rows = jnp.where(ic == 0, rows, rows[::-1]).reshape(NC * NMP, tokens // NMP, 128)
    rows = jnp.pad(rows, ((0, 0), (0, 2), (0, 0)))
    dots = dot_down_sums(pos, g_own, g_other, after(act, other_terms), tile_down).reshape(NMP, NC, 1, 128)
    dots = dots.swapaxes(0, 1).reshape(NC * NMP, 1, 128)
    terms = grad_in_terms(pos, pre_grads, tiles, 0, after(from_other, rows, dots))
    over_z = lax.psum_scatter(terms, "z")
    rows = sum_parts(after(rows, terms), CMP)
    rows = jnp.broadcast_to(rows[None, :6], (NC * NMP, 6, 128))
    rows = exchange(jnp.concatenate([rows, dots, jnp.zeros_like(dots)], axis=1), CMP)
    right_gu_parts = [
        lax.dot_general(proj_gu[:, 32 * k : 32 * k + 32], pre_grads[k], TN, preferred_element_type=F32)
        for k in range(2)
    ]
    left_down_part = lax.dot_general(rows_down.astype(BF16), act, TN, preferred_element_type=F32)
    mine = jnp.concatenate(
        [2.0 * p for p in right_gu_parts] + [2.0 * left_down_part, jnp.pad(dot_gu, ((0, 30), (0, 0)))]
    )
    dots = jnp.sum(rows[:, 6:7], axis=0)
    dots = jnp.concatenate([jnp.where(ic == c, dots, 0.0) for c in range(NC)], axis=1)
    rows = lax.dynamic_slice_in_dim(rows[:, :6], ic * NMP, NMP, 0).reshape(tokens, 128).astype(BF16)
    own = iy * NZ + iz
    own_scale = lax.dynamic_index_in_dim(scale_down, own, 0, keepdims=False)
    own_norm = lax.dynamic_index_in_dim(norm_down, own, 0, keepdims=False)
    own_grads = (out_grad.astype(F32) * own_scale).astype(BF16)
    left_gu_part = lax.dot_general(rows[:, :64], inputs, TN, preferred_element_type=F32)
    right_down_part = lax.dot_general(rows[:, 64:96], own_grads, TN, preferred_element_type=F32)

    cores = [jnp.where(ic == c, mine, 0.0) for c in range(NC)]
    sums = jnp.concatenate(
        [2.0 * left_gu_part, 2.0 * right_down_part, jnp.pad(dots, ((0, 31), (0, 0)))] + cores
    )
    sums = sum_parts(sums.reshape(NDP, 48, width), DP)
    over_z = after(over_z, sums)
    over_z = jnp.roll(over_z, 1 - iy, 0)
    grad_in = over_z[1].astype(F32)
    for p in (0, 2, 3):
        grad_in += step(over_z[p], "y", NY, p - 1).astype(F32)
    sums = gather_small(sums, DP, NDP).reshape(384, width)
    cores = sums[128:].reshape(NC, 128, hidden).swapaxes(0, 1).reshape(128, NC * hidden)
    return (
        grad_in.astype(BF16),
        cores[96:98],
        sums[:64].reshape(2, 32, width).swapaxes(1, 2),
        cores[:64].reshape(2, 32, NC * hidden),
        sums[96] / own_norm[0],
        cores[64:96].T,
        sums[64:96],
    )


def solution(mesh):
    fine = Mesh(mesh.devices.reshape(NX, NC, NY, NZ), ("x", "core", "y", "z"))
    in_specs = (
        P(DP, MP),
        P(DP, MP),
        P(None, DP, MP),
        P(),
        P(None, None, MP),
        P(None, MP),
        P(MP, None),
        P(MP, None),
        P(),
        P(),
    )
    out_specs = (
        P(DP, MP),
        P(None, MP),
        P(None, MP, None),
        P(None, None, MP),
        P(MP),
        P(MP, None),
        P(None, MP),
    )
    return jax.shard_map(shards, mesh=fine, in_specs=in_specs, out_specs=out_specs, check_vma=False)
```

```python
import functools

import jax
import jax.numpy as jnp
from jax import lax
from jax.experimental import pallas as pl
from jax.experimental.pallas import tpu as pltpu
from jax.sharding import Mesh, PartitionSpec as P

F32, BF16 = jnp.float32, jnp.bfloat16
DP, MP, CMP = ("x", "core"), ("y", "z"), ("core", "y", "z")
NX, NC, NY, NZ = 4, 2, 4, 8
NDP, NMP = NX * NC, NY * NZ
NT = (((1,), (1,)), ((), ()))
TN = (((0,), (0,)), ((), ()))
OTHER = [(0, 1), (1, 0)]
VMEM = 50 * 1024 * 1024


def step(array, axis, n, shift):
    return lax.ppermute(array, axis, [(i, (i + shift) % n) for i in range(n)])


def both_ways(a, b, axis, n):
    return step(a, axis, n, 1), step(b, axis, n, -1)


def nothing(*refs):
    pass


def after(array, *others):
    anywhere = pl.BlockSpec(memory_space=pl.ANY)
    return pl.pallas_call(
        nothing,
        in_specs=[anywhere] * (1 + len(others)),
        out_specs=anywhere,
        out_shape=jax.ShapeDtypeStruct(array.shape, array.dtype),
        input_output_aliases={0: 0},
        name="after",
    )(array, *others)


def stack_body(*refs):
    *pieces, first, second, out = refs
    for i, piece in enumerate(pieces):
        out[i] = piece[...]
    half = first.shape[0]
    out[len(pieces), :half] = first[...]
    out[len(pieces), half:] = second[...]


def stack(pieces, first, second):
    return pl.pallas_call(
        stack_body,
        out_shape=jax.ShapeDtypeStruct((len(pieces) + 1,) + pieces[0].shape, BF16),
        compiler_params=pltpu.CompilerParams(vmem_limit_bytes=VMEM),
        cost_estimate=pl.CostEstimate(flops=0, bytes_accessed=6_000_000, transcendentals=0),
        name="stack",
    )(*pieces, first, second)


def rel(a, b, shift, n):
    return lax.rem(a - b + shift + n, n)


def call(body, name, grid, in_specs, out_specs, out_shape, aliases=None):
    return pl.pallas_call(
        body,
        grid_spec=pltpu.PrefetchScalarGridSpec(
            num_scalar_prefetch=1, grid=grid, in_specs=in_specs, out_specs=out_specs
        ),
        out_shape=out_shape,
        input_output_aliases=aliases or {},
        compiler_params=pltpu.CompilerParams(vmem_limit_bytes=VMEM),
        cost_estimate=pl.CostEstimate(flops=1_000_000_000, bytes_accessed=16_000_000, transcendentals=0),
        name=name,
    )


def merge_down_body(pos_ref, frozen_ref, left_ref, right_ref, tile_ref, squares_ref):
    merged = frozen_ref[...].astype(F32) + 2.0 * lax.dot_general(
        left_ref[...], right_ref[...], TN, preferred_element_type=F32
    )
    tile_ref[...] = merged.astype(BF16)
    rows, cols = merged.shape
    squares = jnp.sum((merged * merged).reshape(rows // 8, 8, cols), axis=0)
    for i in range(cols // 128):
        squares_ref[i] = squares[:, i * 128 : (i + 1) * 128]


def merge_down(pos, frozen, left, right):
    f, d = frozen.shape[0] // NC, frozen.shape[1]
    w = d // NY
    return call(
        merge_down_body,
        "merge_down",
        (NY,),
        [
            pl.BlockSpec((f, w), lambda i, p: (p[1], i)),
            pl.BlockSpec((32, f), lambda i, p: (0, p[1])),
            pl.BlockSpec((32, w), lambda i, p: (0, i)),
        ],
        [
            pl.BlockSpec((f, w), lambda i, p: (0, i)),
            pl.BlockSpec((w // 128, 8, 128), lambda i, p: (i, 0, 0)),
        ],
        [
            jax.ShapeDtypeStruct((f, d), BF16),
            jax.ShapeDtypeStruct((d // 128, 8, 128), F32),
        ],
    )(pos, frozen, left, right)


def x_spec(t, w):
    return pl.BlockSpec((1, NZ, t, w), lambda i, p: (rel(i, p[2], 1, NY), 0, 0, 0))


def g_spec(t, w):
    return pl.BlockSpec((NZ, 1, t, w), lambda i, p: (0, rel(i, p[2], 1, NY), 0, 0))


def proj_body(pos_ref, own_ref, other_ref, left_ref, _, out_ref):
    @pl.when(pl.program_id(0) == 0)
    def _():
        out_ref[...] = jnp.zeros_like(out_ref)

    total = jnp.zeros(out_ref.shape, F32)
    for i in range(NZ):
        x = jnp.concatenate([own_ref[0, i], other_ref[0, i]])
        cols = slice(i * 256, (i + 1) * 256)
        left = jnp.concatenate([left_ref[0, :, cols], left_ref[1, :, cols]])
        total += lax.dot_general(x, left, NT, preferred_element_type=F32)
    out_ref[...] += total


def proj_gate_up(pos, own, other, left, before):
    _, _, t, w = own.shape
    return call(
        proj_body,
        "proj_gate_up",
        (NY,),
        [
            x_spec(t, w),
            x_spec(t, w),
            pl.BlockSpec((2, 32, NZ * w), lambda i, p: (0, 0, i)),
            pl.BlockSpec(memory_space=pl.ANY),
        ],
        pl.BlockSpec((2 * t, 64), lambda i, p: (0, 0)),
        jax.ShapeDtypeStruct((2 * t, 64), F32),
    )(pos, own, other, left, before)


def grad_act_body(pos_ref, own_ref, other_ref, scale_ref, tile_ref, right_ref, _, out_ref, rows_ref):
    @pl.when(pl.program_id(0) == 0)
    def _():
        out_ref[...] = jnp.zeros_like(out_ref)
        rows_ref[...] = jnp.zeros_like(rows_ref)

    total, rows = jnp.zeros(out_ref.shape, F32), jnp.zeros(rows_ref.shape, F32)
    for i in range(NZ):
        q = rel(i, pos_ref[3], 3, NZ)
        g = jnp.concatenate([own_ref[q, 0], other_ref[q, 0]]).astype(F32)
        g = (g * scale_ref[i]).astype(BF16)
        cols = slice(i * 256, (i + 1) * 256)
        total += lax.dot_general(g, tile_ref[:, cols], NT, preferred_element_type=F32)
        rows += lax.dot_general(g, right_ref[:, cols], NT, preferred_element_type=F32)
    out_ref[...] += total
    rows_ref[...] += rows


def grad_act_rows(pos, own, other, scale, tile, right, before):
    _, _, t, w = own.shape
    f, d = tile.shape
    return call(
        grad_act_body,
        "grad_act",
        (NY,),
        [
            g_spec(t, w),
            g_spec(t, w),
            pl.BlockSpec((NZ, 1, w), lambda i, p: (i, 0, 0)),
            pl.BlockSpec((f, NZ * w), lambda i, p: (0, i)),
            pl.BlockSpec((32, NZ * w), lambda i, p: (0, i)),
            pl.BlockSpec(memory_space=pl.ANY),
        ],
        [
            pl.BlockSpec((2 * t, f), lambda i, p: (0, 0)),
            pl.BlockSpec((2 * t, 32), lambda i, p: (0, 0)),
        ],
        [jax.ShapeDtypeStruct((2 * t, f), F32), jax.ShapeDtypeStruct((2 * t, 32), F32)],
    )(pos, own, other, scale, tile, right, before)


def dot_down_body(pos_ref, own_ref, other_ref, act_ref, tile_ref, out_ref):
    act = act_ref[...]
    for i in range(NZ):
        q = rel(i, pos_ref[3], 3, NZ)
        g = jnp.concatenate([own_ref[q, 0], other_ref[q, 0]]).astype(F32)
        out_pre = jnp.dot(act, tile_ref[:, i * 256 : (i + 1) * 256], preferred_element_type=F32)
        sums = jnp.sum(g * out_pre, axis=0, keepdims=True)
        out_ref[2 * i] = sums[:, :128]
        out_ref[2 * i + 1] = sums[:, 128:]


def dot_down_sums(pos, own, other, act, tile):
    _, _, t, w = own.shape
    f, d = tile.shape
    return call(
        dot_down_body,
        "dot_down",
        (NY,),
        [
            g_spec(t, w),
            g_spec(t, w),
            pl.BlockSpec((2 * t, f), lambda i, p: (0, 0)),
            pl.BlockSpec((f, NZ * w), lambda i, p: (0, i)),
        ],
        pl.BlockSpec((2 * NZ, 1, 128), lambda i, p: (i, 0, 0)),
        jax.ShapeDtypeStruct((2 * NMP, 1, 128), F32),
    )(pos, own, other, act, tile)


def gate_up_body(
    pos_ref, own_ref, other_ref, frozen_ref, left_ref, right_ref, _, tile_ref, pre_ref, squares_ref
):
    @pl.when(pl.program_id(0) == 0)
    def _():
        pre_ref[...] = jnp.zeros_like(pre_ref)
        squares_ref[...] = jnp.zeros_like(squares_ref)

    for k in range(2):
        right = right_ref[k]
        pre, squares = jnp.zeros(pre_ref.shape[1:], F32), jnp.zeros(squares_ref.shape[1:], F32)
        for i in range(NZ):
            x = jnp.concatenate([own_ref[0, i], other_ref[0, i]])
            rows = slice(i * 256, (i + 1) * 256)
            merged = frozen_ref[k, rows].astype(F32) + 2.0 * lax.dot_general(
                left_ref[k, :, rows], right, TN, preferred_element_type=F32
            )
            tile = merged.astype(BF16)
            tile_ref[k, rows] = tile
            squares += jnp.sum((merged * merged).reshape(32, 8, -1), axis=0)
            pre += jnp.dot(x, tile, preferred_element_type=F32)
        pre_ref[k] += pre
        squares_ref[k] += squares


def gate_up(pos, own, other, frozen, left, right, before):
    _, _, t, w = own.shape
    _, d, f = frozen.shape
    f, rows = f // NC, NZ * w
    return call(
        gate_up_body,
        "gate_up",
        (NY,),
        [
            x_spec(t, w),
            x_spec(t, w),
            pl.BlockSpec((2, rows, f), lambda i, p: (0, i, p[1])),
            pl.BlockSpec((2, 32, rows), lambda i, p: (0, 0, i)),
            pl.BlockSpec((2, 32, f), lambda i, p: (0, 0, 0)),
            pl.BlockSpec(memory_space=pl.ANY),
        ],
        [
            pl.BlockSpec((2, rows, f), lambda i, p: (0, i, 0)),
            pl.BlockSpec((2, 2 * t, f), lambda i, p: (0, 0, 0)),
            pl.BlockSpec((2, 8, f), lambda i, p: (0, 0, 0)),
        ],
        [
            jax.ShapeDtypeStruct((2, d, f), BF16),
            jax.ShapeDtypeStruct((2, 2 * t, f), F32),
            jax.ShapeDtypeStruct((2, 8, f), F32),
        ],
    )(pos, own, other, frozen, left, right, before)


def grad_in_body(pos_ref, grads_ref, tile_ref, own_ref, other_ref):
    t = grads_ref.shape[1] // 2
    for i in range(NZ):
        rows = slice(i * 256, (i + 1) * 256)
        out = lax.dot_general(grads_ref[0], tile_ref[0, rows], NT, preferred_element_type=F32)
        out += lax.dot_general(grads_ref[1], tile_ref[1, rows], NT, preferred_element_type=F32)
        out = out.astype(BF16)
        own_ref[i, 0] = out[:t]
        other_ref[i, 0] = out[t:]


def grad_in_parts(pos, grads, tiles):
    _, t, f = grads.shape
    out = pl.BlockSpec((NZ, 1, t // 2, 256), lambda i, p: (0, i, 0, 0))
    shape = jax.ShapeDtypeStruct((NZ, NY, t // 2, 256), BF16)
    return call(
        grad_in_body,
        "grad_in",
        (NY,),
        [
            pl.BlockSpec((2, t, f), lambda i, p: (0, 0, 0)),
            pl.BlockSpec((2, NZ * 256, f), lambda i, p: (0, i, 0)),
        ],
        [out, out],
        [shape, shape],
    )(pos, grads, tiles)


def exchange(parts, axes):
    return lax.all_to_all(parts, axes, 0, 0, tiled=True)


def sum_parts(parts, axes):
    return jnp.sum(exchange(parts, axes).astype(F32), axis=0)


def gather_small(own, axes, n):
    return exchange(jnp.broadcast_to(own[None], (n,) + own.shape), axes)


def shards(
    inputs,
    out_grad,
    frozen_gu,
    left_gu,
    right_gu,
    magnitude_gu,
    frozen_down,
    left_down,
    right_down,
    magnitude_down,
):
    tokens, width = inputs.shape
    hidden = frozen_gu.shape[2] // NC
    ix, ic, iy, iz = (lax.axis_index(a) for a in ("x", "core", "y", "z"))
    pos = jnp.stack([ix, ic, iy, iz]).astype(jnp.int32)

    def half_of(array, core, axis):
        return lax.dynamic_slice_in_dim(array, core * hidden, hidden, axis)

    frozen_full = lax.all_gather(frozen_gu, DP, axis=1, tiled=True)
    g_y = jnp.stack(
        [step(out_grad, "y", NY, 1), out_grad, step(out_grad, "y", NY, -1), step(out_grad, "y", NY, 2)]
    )
    x_z = gather_small(inputs, "z", NZ)
    tile_down, down_squares = merge_down(pos, frozen_down, left_down.T, right_down)
    x_z = after(x_z, down_squares)
    yr, yl = both_ways(x_z, x_z, "y", NY)
    yfr, yfl = both_ways(yr[: NZ // 2], yl[NZ // 2 :], "y", NY)
    x_own = stack([yr, x_z, yl], yfr, yfl)
    r1, l1 = both_ways(g_y, g_y, "z", NZ)
    down_sum = jnp.sum(sum_parts(after(down_squares, r1, l1), CMP), axis=0, keepdims=True)
    r2, l2 = both_ways(r1, l1, "z", NZ)
    r2, l2 = after(r2, down_sum), after(l2, down_sum)
    down_sums = gather_small(jnp.broadcast_to(down_sum, (8, 128)), CMP, NC * NMP)[:, :1]
    r3, l3 = both_ways(r2, l2, "z", NZ)
    r3, l3 = after(r3, down_sums), after(l3, down_sums)
    zfr, zfl = both_ways(r3[: NY // 2], l3[NY // 2 :], "z", NZ)
    g_own = stack([r3, r2, r1, g_y, l1, l2, l3], zfr, zfl)
    x_other = lax.ppermute(x_own, "core", OTHER)
    g_other = lax.ppermute(g_own, "core", OTHER)
    right = half_of(right_gu, ic, 2)
    left_t = left_gu.swapaxes(1, 2)

    norm_down = jnp.sqrt(down_sums.reshape(NMP, 1, width) + 1e-06)
    scale_down = magnitude_down.reshape(NMP, 1, width) / norm_down

    tiles, pre_gu, squares = gate_up(pos, x_own, x_other, frozen_full, left_t, right, down_sums)
    grad_act, rows_down = grad_act_rows(pos, g_own, g_other, scale_down, tile_down, right_down, squares)
    norm_gu = jnp.sqrt(jnp.sum(squares, axis=1) + 1e-06)
    scale_gu = half_of(magnitude_gu, ic, 1) / norm_gu
    hid_gu = pre_gu * scale_gu[:, None, :]
    sig = jax.nn.sigmoid(hid_gu[0])
    silu_gate = hid_gu[0] * sig
    act = (silu_gate * hid_gu[1]).astype(BF16)
    grad_gate = grad_act * hid_gu[1] * sig * (1.0 + hid_gu[0] * (1.0 - sig))
    grad_up = grad_act * silu_gate
    grad_hid = jnp.stack([grad_gate, grad_up])
    dot_gu = jnp.sum(grad_hid * pre_gu, axis=1) / norm_gu
    pre_grads = (grad_hid * scale_gu[:, None, :]).astype(BF16)

    own_terms, other_terms = grad_in_parts(pos, pre_grads, tiles)
    from_other = lax.ppermute(other_terms, "core", OTHER)

    rows_gu = [
        lax.dot_general(pre_grads[k], right[k], NT, preferred_element_type=F32) for k in range(2)
    ]
    proj_down = jnp.dot(act, half_of(left_down, ic, 0), preferred_element_type=F32)
    rows = jnp.concatenate(rows_gu + [proj_down, jnp.zeros_like(proj_down)], axis=1)
    rows = rows.reshape(NC, NMP, tokens // NMP, 128)
    rows = jnp.where(ic == 0, rows, rows[::-1]).reshape(NC * NMP, tokens // NMP, 128)
    rows = jnp.pad(rows, ((0, 0), (0, 2), (0, 0)))
    from_other = after(from_other, rows)
    terms = (own_terms.astype(F32) + from_other.astype(F32)).astype(BF16)
    over_z = lax.psum_scatter(terms, "z")
    rows = sum_parts(rows, CMP)
    dots = dot_down_sums(pos, g_own, g_other, act, tile_down).reshape(NMP, NC, 1, 128)
    dots = dots.swapaxes(0, 1).reshape(NC * NMP, 1, 128)
    rows_sum = rows
    rows = jnp.broadcast_to(rows[None, :6], (NC * NMP, 6, 128))
    rows = exchange(jnp.concatenate([rows, dots, jnp.zeros_like(dots)], axis=1), CMP)
    proj_gu = proj_gate_up(pos, x_own, x_other, left_t, rows_sum).astype(BF16)
    right_gu_parts = [
        lax.dot_general(proj_gu[:, 32 * k : 32 * k + 32], pre_grads[k], TN, preferred_element_type=F32)
        for k in range(2)
    ]
    left_down_part = lax.dot_general(rows_down.astype(BF16), act, TN, preferred_element_type=F32)
    mine = jnp.concatenate(
        [2.0 * p for p in right_gu_parts] + [2.0 * left_down_part, jnp.pad(dot_gu, ((0, 30), (0, 0)))]
    )
    dots = jnp.sum(rows[:, 6:7], axis=0)
    dots = jnp.concatenate([jnp.where(ic == c, dots, 0.0) for c in range(NC)], axis=1)
    rows = lax.dynamic_slice_in_dim(rows[:, :6], ic * NMP, NMP, 0).reshape(tokens, 128).astype(BF16)
    own = iy * NZ + iz
    own_scale = lax.dynamic_index_in_dim(scale_down, own, 0, keepdims=False)
    own_norm = lax.dynamic_index_in_dim(norm_down, own, 0, keepdims=False)
    own_grads = (out_grad.astype(F32) * own_scale).astype(BF16)
    left_gu_part = lax.dot_general(rows[:, :64], inputs, TN, preferred_element_type=F32)
    right_down_part = lax.dot_general(rows[:, 64:96], own_grads, TN, preferred_element_type=F32)

    cores = [jnp.where(ic == c, mine, 0.0) for c in range(NC)]
    sums = jnp.concatenate(
        [2.0 * left_gu_part, 2.0 * right_down_part, jnp.pad(dots, ((0, 31), (0, 0)))] + cores
    )
    sums = sum_parts(sums.reshape(NDP, 48, width), DP)
    over_z = jnp.roll(after(over_z, sums), 1 - iy, 0)
    sent = [step(over_z[p], "y", NY, p - 1) for p in (0, 2, 3)]
    grad_in = over_z[1].astype(F32) + sum(r.astype(F32) for r in sent)
    sums = after(gather_small(sums, DP, NDP), *sent).reshape(384, width)
    cores = sums[128:].reshape(NC, 128, hidden).swapaxes(0, 1).reshape(128, NC * hidden)
    return (
        grad_in.astype(BF16),
        cores[96:98],
        sums[:64].reshape(2, 32, width).swapaxes(1, 2),
        cores[:64].reshape(2, 32, NC * hidden),
        sums[96] / own_norm[0],
        cores[64:96].T,
        sums[64:96],
    )


def solution(mesh):
    fine = Mesh(mesh.devices.reshape(NX, NC, NY, NZ), ("x", "core", "y", "z"))
    in_specs = (
        P(DP, MP),
        P(DP, MP),
        P(None, DP, MP),
        P(),
        P(None, None, MP),
        P(None, MP),
        P(MP, None),
        P(MP, None),
        P(),
        P(),
    )
    out_specs = (
        P(DP, MP),
        P(None, MP),
        P(None, MP, None),
        P(None, None, MP),
        P(MP),
        P(MP, None),
        P(None, MP),
    )
    return jax.shard_map(shards, mesh=fine, in_specs=in_specs, out_specs=out_specs, check_vma=False)
```

```python
import functools

import jax
import jax.numpy as jnp
from jax import lax
from jax.experimental import pallas as pl
from jax.experimental.pallas import tpu as pltpu
from jax.sharding import Mesh, PartitionSpec as P

F32, BF16 = jnp.float32, jnp.bfloat16
DP, MP, CMP = ("x", "core"), ("y", "z"), ("core", "y", "z")
NX, NC, NY, NZ = 4, 2, 4, 8
NDP, NMP = NX * NC, NY * NZ
NT = (((1,), (1,)), ((), ()))
TN = (((0,), (0,)), ((), ()))
OTHER = [(0, 1), (1, 0)]
VMEM = 50 * 1024 * 1024


def step(array, axis, n, shift):
    return lax.ppermute(array, axis, [(i, (i + shift) % n) for i in range(n)])


def both_ways(a, b, axis, n):
    return step(a, axis, n, 1), step(b, axis, n, -1)


def nothing(*refs):
    pass


def after(array, *others):
    anywhere = pl.BlockSpec(memory_space=pl.ANY)
    return pl.pallas_call(
        nothing,
        in_specs=[anywhere] * (1 + len(others)),
        out_specs=anywhere,
        out_shape=jax.ShapeDtypeStruct(array.shape, array.dtype),
        input_output_aliases={0: 0},
        name="after",
    )(array, *others)


def stack_body(*refs):
    *pieces, first, second, out = refs
    for i, piece in enumerate(pieces):
        out[i] = piece[...]
    half = first.shape[0]
    out[len(pieces), :half] = first[...]
    out[len(pieces), half:] = second[...]


def stack(pieces, first, second):
    return pl.pallas_call(
        stack_body,
        out_shape=jax.ShapeDtypeStruct((len(pieces) + 1,) + pieces[0].shape, BF16),
        compiler_params=pltpu.CompilerParams(vmem_limit_bytes=VMEM),
        cost_estimate=pl.CostEstimate(flops=0, bytes_accessed=6_000_000, transcendentals=0),
        name="stack",
    )(*pieces, first, second)


def rel(a, b, shift, n):
    return lax.rem(a - b + shift + n, n)


def call(body, name, grid, in_specs, out_specs, out_shape, aliases=None):
    return pl.pallas_call(
        body,
        grid_spec=pltpu.PrefetchScalarGridSpec(
            num_scalar_prefetch=1, grid=grid, in_specs=in_specs, out_specs=out_specs
        ),
        out_shape=out_shape,
        input_output_aliases=aliases or {},
        compiler_params=pltpu.CompilerParams(vmem_limit_bytes=VMEM),
        cost_estimate=pl.CostEstimate(flops=1_000_000_000, bytes_accessed=16_000_000, transcendentals=0),
        name=name,
    )


def merge_down_body(pos_ref, frozen_ref, left_ref, right_ref, tile_ref, squares_ref):
    merged = frozen_ref[...].astype(F32) + 2.0 * lax.dot_general(
        left_ref[...], right_ref[...], TN, preferred_element_type=F32
    )
    tile_ref[...] = merged.astype(BF16)
    rows, cols = merged.shape
    squares = jnp.sum((merged * merged).reshape(rows // 8, 8, cols), axis=0)
    for i in range(cols // 128):
        squares_ref[i] = squares[:, i * 128 : (i + 1) * 128]


def merge_down(pos, frozen, left, right):
    f, d = frozen.shape[0] // NC, frozen.shape[1]
    w = d // NY
    return call(
        merge_down_body,
        "merge_down",
        (NY,),
        [
            pl.BlockSpec((f, w), lambda i, p: (p[1], i)),
            pl.BlockSpec((32, f), lambda i, p: (0, p[1])),
            pl.BlockSpec((32, w), lambda i, p: (0, i)),
        ],
        [
            pl.BlockSpec((f, w), lambda i, p: (0, i)),
            pl.BlockSpec((w // 128, 8, 128), lambda i, p: (i, 0, 0)),
        ],
        [
            jax.ShapeDtypeStruct((f, d), BF16),
            jax.ShapeDtypeStruct((d // 128, 8, 128), F32),
        ],
    )(pos, frozen, left, right)


def x_spec(t, w):
    return pl.BlockSpec((1, NZ, t, w), lambda i, p: (rel(i, p[2], 1, NY), 0, 0, 0))


def g_spec(t, w):
    return pl.BlockSpec((NZ, 1, t, w), lambda i, p: (0, rel(i, p[2], 1, NY), 0, 0))


def proj_body(pos_ref, own_ref, other_ref, left_ref, _, out_ref):
    @pl.when(pl.program_id(0) == 0)
    def _():
        out_ref[...] = jnp.zeros_like(out_ref)

    total = jnp.zeros(out_ref.shape, F32)
    for i in range(NZ):
        x = jnp.concatenate([own_ref[0, i], other_ref[0, i]])
        cols = slice(i * 256, (i + 1) * 256)
        left = jnp.concatenate([left_ref[0, :, cols], left_ref[1, :, cols]])
        total += lax.dot_general(x, left, NT, preferred_element_type=F32)
    out_ref[...] += total


def proj_gate_up(pos, own, other, left, before):
    _, _, t, w = own.shape
    return call(
        proj_body,
        "proj_gate_up",
        (NY,),
        [
            x_spec(t, w),
            x_spec(t, w),
            pl.BlockSpec((2, 32, NZ * w), lambda i, p: (0, 0, i)),
            pl.BlockSpec(memory_space=pl.ANY),
        ],
        pl.BlockSpec((2 * t, 64), lambda i, p: (0, 0)),
        jax.ShapeDtypeStruct((2 * t, 64), F32),
    )(pos, own, other, left, before)


def grad_act_body(pos_ref, own_ref, other_ref, scale_ref, tile_ref, right_ref, _, out_ref, rows_ref):
    @pl.when(pl.program_id(0) == 0)
    def _():
        out_ref[...] = jnp.zeros_like(out_ref)
        rows_ref[...] = jnp.zeros_like(rows_ref)

    total, rows = jnp.zeros(out_ref.shape, F32), jnp.zeros(rows_ref.shape, F32)
    for i in range(NZ):
        q = rel(i, pos_ref[3], 3, NZ)
        g = jnp.concatenate([own_ref[q, 0], other_ref[q, 0]]).astype(F32)
        g = (g * scale_ref[i]).astype(BF16)
        cols = slice(i * 256, (i + 1) * 256)
        total += lax.dot_general(g, tile_ref[:, cols], NT, preferred_element_type=F32)
        rows += lax.dot_general(g, right_ref[:, cols], NT, preferred_element_type=F32)
    out_ref[...] += total
    rows_ref[...] += rows


def grad_act_rows(pos, own, other, scale, tile, right, before):
    _, _, t, w = own.shape
    f, d = tile.shape
    return call(
        grad_act_body,
        "grad_act",
        (NY,),
        [
            g_spec(t, w),
            g_spec(t, w),
            pl.BlockSpec((NZ, 1, w), lambda i, p: (i, 0, 0)),
            pl.BlockSpec((f, NZ * w), lambda i, p: (0, i)),
            pl.BlockSpec((32, NZ * w), lambda i, p: (0, i)),
            pl.BlockSpec(memory_space=pl.ANY),
        ],
        [
            pl.BlockSpec((2 * t, f), lambda i, p: (0, 0)),
            pl.BlockSpec((2 * t, 32), lambda i, p: (0, 0)),
        ],
        [jax.ShapeDtypeStruct((2 * t, f), F32), jax.ShapeDtypeStruct((2 * t, 32), F32)],
    )(pos, own, other, scale, tile, right, before)


def dot_down_body(pos_ref, own_ref, other_ref, act_ref, tile_ref, out_ref):
    act = act_ref[...]
    for i in range(NZ):
        q = rel(i, pos_ref[3], 3, NZ)
        g = jnp.concatenate([own_ref[q, 0], other_ref[q, 0]]).astype(F32)
        out_pre = jnp.dot(act, tile_ref[:, i * 256 : (i + 1) * 256], preferred_element_type=F32)
        sums = jnp.sum(g * out_pre, axis=0, keepdims=True)
        out_ref[2 * i] = sums[:, :128]
        out_ref[2 * i + 1] = sums[:, 128:]


def dot_down_sums(pos, own, other, act, tile):
    _, _, t, w = own.shape
    f, d = tile.shape
    return call(
        dot_down_body,
        "dot_down",
        (NY,),
        [
            g_spec(t, w),
            g_spec(t, w),
            pl.BlockSpec((2 * t, f), lambda i, p: (0, 0)),
            pl.BlockSpec((f, NZ * w), lambda i, p: (0, i)),
        ],
        pl.BlockSpec((2 * NZ, 1, 128), lambda i, p: (i, 0, 0)),
        jax.ShapeDtypeStruct((2 * NMP, 1, 128), F32),
    )(pos, own, other, act, tile)


def gate_up_body(
    pos_ref, own_ref, other_ref, frozen_ref, left_ref, right_ref, _, tile_ref, pre_ref, squares_ref
):
    @pl.when(pl.program_id(0) == 0)
    def _():
        pre_ref[...] = jnp.zeros_like(pre_ref)
        squares_ref[...] = jnp.zeros_like(squares_ref)

    for k in range(2):
        right = right_ref[k]
        pre, squares = jnp.zeros(pre_ref.shape[1:], F32), jnp.zeros(squares_ref.shape[1:], F32)
        for i in range(NZ):
            x = jnp.concatenate([own_ref[0, i], other_ref[0, i]])
            rows = slice(i * 256, (i + 1) * 256)
            merged = frozen_ref[k, rows].astype(F32) + 2.0 * lax.dot_general(
                left_ref[k, :, rows], right, TN, preferred_element_type=F32
            )
            tile = merged.astype(BF16)
            tile_ref[k, rows] = tile
            squares += jnp.sum((merged * merged).reshape(32, 8, -1), axis=0)
            pre += jnp.dot(x, tile, preferred_element_type=F32)
        pre_ref[k] += pre
        squares_ref[k] += squares


def gate_up(pos, own, other, frozen, left, right, before):
    _, _, t, w = own.shape
    _, d, f = frozen.shape
    f, rows = f // NC, NZ * w
    return call(
        gate_up_body,
        "gate_up",
        (NY,),
        [
            x_spec(t, w),
            x_spec(t, w),
            pl.BlockSpec((2, rows, f), lambda i, p: (0, i, p[1])),
            pl.BlockSpec((2, 32, rows), lambda i, p: (0, 0, i)),
            pl.BlockSpec((2, 32, f), lambda i, p: (0, 0, 0)),
            pl.BlockSpec(memory_space=pl.ANY),
        ],
        [
            pl.BlockSpec((2, rows, f), lambda i, p: (0, i, 0)),
            pl.BlockSpec((2, 2 * t, f), lambda i, p: (0, 0, 0)),
            pl.BlockSpec((2, 8, f), lambda i, p: (0, 0, 0)),
        ],
        [
            jax.ShapeDtypeStruct((2, d, f), BF16),
            jax.ShapeDtypeStruct((2, 2 * t, f), F32),
            jax.ShapeDtypeStruct((2, 8, f), F32),
        ],
    )(pos, own, other, frozen, left, right, before)


def grad_in_body(pos_ref, grads_ref, tile_ref, own_ref, other_ref):
    t = grads_ref.shape[1] // 2
    for i in range(NZ):
        rows = slice(i * 256, (i + 1) * 256)
        out = lax.dot_general(grads_ref[0], tile_ref[0, rows], NT, preferred_element_type=F32)
        out += lax.dot_general(grads_ref[1], tile_ref[1, rows], NT, preferred_element_type=F32)
        out = out.astype(BF16)
        own_ref[i, 0] = out[:t]
        other_ref[i, 0] = out[t:]


def grad_in_parts(pos, grads, tiles):
    _, t, f = grads.shape
    out = pl.BlockSpec((NZ, 1, t // 2, 256), lambda i, p: (0, i, 0, 0))
    shape = jax.ShapeDtypeStruct((NZ, NY, t // 2, 256), BF16)
    return call(
        grad_in_body,
        "grad_in",
        (NY,),
        [
            pl.BlockSpec((2, t, f), lambda i, p: (0, 0, 0)),
            pl.BlockSpec((2, NZ * 256, f), lambda i, p: (0, i, 0)),
        ],
        [out, out],
        [shape, shape],
    )(pos, grads, tiles)


def exchange(parts, axes):
    return lax.all_to_all(parts, axes, 0, 0, tiled=True)


def sum_parts(parts, axes):
    return jnp.sum(exchange(parts, axes).astype(F32), axis=0)


def gather_small(own, axes, n):
    return exchange(jnp.broadcast_to(own[None], (n,) + own.shape), axes)


def shards(
    inputs,
    out_grad,
    frozen_gu,
    left_gu,
    right_gu,
    magnitude_gu,
    frozen_down,
    left_down,
    right_down,
    magnitude_down,
):
    tokens, width = inputs.shape
    hidden = frozen_gu.shape[2] // NC
    ix, ic, iy, iz = (lax.axis_index(a) for a in ("x", "core", "y", "z"))
    pos = jnp.stack([ix, ic, iy, iz]).astype(jnp.int32)

    def half_of(array, core, axis):
        return lax.dynamic_slice_in_dim(array, core * hidden, hidden, axis)

    frozen_full = lax.all_gather(frozen_gu, DP, axis=1, tiled=True)
    g_y = jnp.stack(
        [step(out_grad, "y", NY, 1), out_grad, step(out_grad, "y", NY, -1), step(out_grad, "y", NY, 2)]
    )
    x_z = gather_small(inputs, "z", NZ)
    tile_down, down_squares = merge_down(pos, frozen_down, left_down.T, right_down)
    x_z = after(x_z, down_squares)
    yr, yl = both_ways(x_z, x_z, "y", NY)
    yfr, yfl = both_ways(yr[: NZ // 2], yl[NZ // 2 :], "y", NY)
    x_own = stack([yr, x_z, yl], yfr, yfl)
    r1, l1 = both_ways(g_y, g_y, "z", NZ)
    down_sum = jnp.sum(sum_parts(after(down_squares, r1, l1), CMP), axis=0, keepdims=True)
    r2, l2 = both_ways(r1, l1, "z", NZ)
    r2, l2 = after(r2, down_sum), after(l2, down_sum)
    down_sums = gather_small(jnp.broadcast_to(down_sum, (8, 128)), CMP, NC * NMP)[:, :1]
    r3, l3 = both_ways(r2, l2, "z", NZ)
    r3, l3 = after(r3, down_sums), after(l3, down_sums)
    zfr, zfl = both_ways(r3[: NY // 2], l3[NY // 2 :], "z", NZ)
    g_own = stack([r3, r2, r1, g_y, l1, l2, l3], zfr, zfl)
    x_other = lax.ppermute(x_own, "core", OTHER)
    g_other = lax.ppermute(g_own, "core", OTHER)
    right = half_of(right_gu, ic, 2)
    left_t = left_gu.swapaxes(1, 2)

    norm_down = jnp.sqrt(down_sums.reshape(NMP, 1, width) + 1e-06)
    scale_down = magnitude_down.reshape(NMP, 1, width) / norm_down

    tiles, pre_gu, squares = gate_up(pos, x_own, x_other, frozen_full, left_t, right, down_sums)
    grad_act, rows_down = grad_act_rows(pos, g_own, g_other, scale_down, tile_down, right_down, squares)
    norm_gu = jnp.sqrt(jnp.sum(squares, axis=1) + 1e-06)
    scale_gu = half_of(magnitude_gu, ic, 1) / norm_gu
    hid_gu = pre_gu * scale_gu[:, None, :]
    sig = jax.nn.sigmoid(hid_gu[0])
    silu_gate = hid_gu[0] * sig
    act = (silu_gate * hid_gu[1]).astype(BF16)
    grad_gate = grad_act * hid_gu[1] * sig * (1.0 + hid_gu[0] * (1.0 - sig))
    grad_up = grad_act * silu_gate
    grad_hid = jnp.stack([grad_gate, grad_up])
    dot_gu = jnp.sum(grad_hid * pre_gu, axis=1) / norm_gu
    pre_grads = (grad_hid * scale_gu[:, None, :]).astype(BF16)

    own_terms, other_terms = grad_in_parts(pos, pre_grads, tiles)
    from_other = lax.ppermute(other_terms, "core", OTHER)

    rows_gu = [
        lax.dot_general(pre_grads[k], right[k], NT, preferred_element_type=F32) for k in range(2)
    ]
    proj_down = jnp.dot(act, half_of(left_down, ic, 0), preferred_element_type=F32)
    rows = jnp.concatenate(rows_gu + [proj_down, jnp.zeros_like(proj_down)], axis=1)
    rows = rows.reshape(NC, NMP, tokens // NMP, 128)
    rows = jnp.where(ic == 0, rows, rows[::-1]).reshape(NC * NMP, tokens // NMP, 128)
    rows = jnp.pad(rows, ((0, 0), (0, 2), (0, 0)))
    dots = dot_down_sums(pos, g_own, g_other, act, tile_down).reshape(NMP, NC, 1, 128)
    dots = dots.swapaxes(0, 1).reshape(NC * NMP, 1, 128)
    from_other = after(from_other, rows, dots)
    terms = (own_terms.astype(F32) + from_other.astype(F32)).astype(BF16)
    over_z = lax.psum_scatter(terms, "z")
    rows = sum_parts(rows, CMP)
    rows_sum = rows
    rows = jnp.broadcast_to(rows[None, :6], (NC * NMP, 6, 128))
    rows = exchange(jnp.concatenate([rows, dots, jnp.zeros_like(dots)], axis=1), CMP)
    proj_gu = proj_gate_up(pos, x_own, x_other, left_t, rows_sum).astype(BF16)
    right_gu_parts = [
        lax.dot_general(proj_gu[:, 32 * k : 32 * k + 32], pre_grads[k], TN, preferred_element_type=F32)
        for k in range(2)
    ]
    left_down_part = lax.dot_general(rows_down.astype(BF16), act, TN, preferred_element_type=F32)
    mine = jnp.concatenate(
        [2.0 * p for p in right_gu_parts] + [2.0 * left_down_part, jnp.pad(dot_gu, ((0, 30), (0, 0)))]
    )
    dots = jnp.sum(rows[:, 6:7], axis=0)
    dots = jnp.concatenate([jnp.where(ic == c, dots, 0.0) for c in range(NC)], axis=1)
    rows = lax.dynamic_slice_in_dim(rows[:, :6], ic * NMP, NMP, 0).reshape(tokens, 128).astype(BF16)
    own = iy * NZ + iz
    own_scale = lax.dynamic_index_in_dim(scale_down, own, 0, keepdims=False)
    own_norm = lax.dynamic_index_in_dim(norm_down, own, 0, keepdims=False)
    own_grads = (out_grad.astype(F32) * own_scale).astype(BF16)
    left_gu_part = lax.dot_general(rows[:, :64], inputs, TN, preferred_element_type=F32)
    right_down_part = lax.dot_general(rows[:, 64:96], own_grads, TN, preferred_element_type=F32)

    cores = [jnp.where(ic == c, mine, 0.0) for c in range(NC)]
    sums = jnp.concatenate(
        [2.0 * left_gu_part, 2.0 * right_down_part, jnp.pad(dots, ((0, 31), (0, 0)))] + cores
    )
    sums = sum_parts(sums.reshape(NDP, 48, width), DP)
    over_z = jnp.roll(after(over_z, sums), 1 - iy, 0)
    sent = [step(over_z[p], "y", NY, p - 1) for p in (0, 2, 3)]
    grad_in = over_z[1].astype(F32) + sum(r.astype(F32) for r in sent)
    sums = gather_small(sums, DP, NDP).reshape(384, width)
    cores = sums[128:].reshape(NC, 128, hidden).swapaxes(0, 1).reshape(128, NC * hidden)
    return (
        grad_in.astype(BF16),
        cores[96:98],
        sums[:64].reshape(2, 32, width).swapaxes(1, 2),
        cores[:64].reshape(2, 32, NC * hidden),
        sums[96] / own_norm[0],
        cores[64:96].T,
        sums[64:96],
    )


def solution(mesh):
    fine = Mesh(mesh.devices.reshape(NX, NC, NY, NZ), ("x", "core", "y", "z"))
    in_specs = (
        P(DP, MP),
        P(DP, MP),
        P(None, DP, MP),
        P(),
        P(None, None, MP),
        P(None, MP),
        P(MP, None),
        P(MP, None),
        P(),
        P(),
    )
    out_specs = (
        P(DP, MP),
        P(None, MP),
        P(None, MP, None),
        P(None, None, MP),
        P(MP),
        P(MP, None),
        P(None, MP),
    )
    return jax.shard_map(shards, mesh=fine, in_specs=in_specs, out_specs=out_specs, check_vma=False)
```
